32 devices in a mesh: dp: 4 (over y, x), tensor: 8 (over z, core).
Axes of the slice: x: 2, y: 2, z: 4, core: 2. Of those that a mesh axis runs over, the one named last changes fastest.
Arguments:
- tokens: bfloat16 [2048, 8192], P('dp'), may hold values from -5 to 5
- grad_out: bfloat16 [2048, 768], P('dp', 'tensor'), may hold values from -0.3125 to 0.3125
- feedback: bfloat16 [4, 768, 8192], P('dp', 'tensor'), may hold values from -6 to 6
- q_prev: float32 [8192, 32], replicated, may hold values from -0.0625 to 0.0625
Outputs:
- q_factor: float32 [8192, 32], replicated
- update: bfloat16 [768, 8192], P('tensor')
- new_feedback: bfloat16 [4, 768, 8192], P('dp', 'tensor')
The draws below stay inside these ranges and needn't reach their ends.
All inputs are finite; a program needn't handle non-finite values.
Results may differ from the reference program's by a relative error of at most 0.001.
Values sent between devices are 32-bit elements; how exact they have to be, the bound alone decides.
No kernel may reach another device: no remote copies, remote signals or barrier semaphores. Data moves between devices by JAX's collectives and lax.ppermute only.
A program may use at most 64 MiB of HBM per device.

```python
import jax
import jax.numpy as jnp
from jax import lax

D = 8192
TOK_DEV = 512
R = 32
REPLICAS = 4
TOKENS = 2048
HID_ALL = 768


def draw_tokens(key, part):
    key = jax.random.fold_in(key, 11)
    k_common, k_noise = jax.random.split(key, 2)
    common = jax.random.normal(k_common, (TOK_DEV, D))
    noise = jax.random.normal(k_noise, (REPLICAS, TOK_DEV, D))
    whole = jnp.clip(0.6 * common[None] + 0.8 * noise, -5.0, 5.0)
    return whole.reshape(TOKENS, D).astype(jnp.bfloat16)


def draw_grad_out(key, part):
    key = jax.random.fold_in(key, 23)
    k_common, k_noise = jax.random.split(key, 2)
    common = jax.random.normal(k_common, (TOK_DEV, HID_ALL))
    noise = jax.random.normal(k_noise, (REPLICAS, TOK_DEV, HID_ALL))
    whole = jnp.clip(0.6 * common[None] + 0.8 * noise, -5.0, 5.0) * 0.0625
    return whole.reshape(TOKENS, HID_ALL).astype(jnp.bfloat16)


def block_scale(own_key, extent, cuts, low, high):
    gain = 1.0
    for dim, shards_of in cuts:
        steps = jax.random.uniform(jax.random.fold_in(jax.random.fold_in(own_key, 6), dim), (shards_of,), jnp.float32, low / len(cuts), high / len(cuts))
        gain = gain * jnp.repeat(jnp.exp(steps), extent[dim] // shards_of).reshape((-1,) + (1,) * (len(extent) - 1 - dim))
    return gain


def gaussian(own_key, dims, width, bound, cuts=(), kind=jnp.bfloat16):
    drawn = jax.random.normal(own_key, dims, jnp.float32) * width
    if len(cuts) > 0:
        drawn = block_scale(own_key, dims, cuts, -0.22, 0.18) * drawn
    return jnp.clip(drawn, min=-bound, max=bound).astype(kind)


def setup_inputs(seed: int = 0) -> dict:
    key_list = jax.random.split(jax.random.key(seed), 5)
    return {
        "tokens": draw_tokens(jax.random.fold_in(key_list[4], 71), 0),
        "grad_out": draw_grad_out(jax.random.fold_in(key_list[4], 71), 0),
        "feedback": gaussian(key_list[2], (REPLICAS, HID_ALL, D), 1.0, 6.0, ((0, 4), (1, 8))),
        "q_prev": gaussian(key_list[3], (D, R), D ** -0.5, 0.0625, (), jnp.float32),
    }


def reference(tokens, grad_out, feedback, q_prev):
    highest = lax.Precision.HIGHEST
    acts = tokens.reshape(REPLICAS, TOK_DEV, D)
    grads = grad_out.reshape(REPLICAS, TOK_DEV, HID_ALL)
    contract = (((0,), (0,)), ((), ()))

    def add_p(carry, index):
        proj = jnp.dot(acts[index].astype(jnp.float32), q_prev, precision=highest)
        term = lax.dot_general(grads[index].astype(jnp.float32), proj, contract, precision=highest)
        term = term + jnp.dot(feedback[index].astype(jnp.float32), q_prev, precision=highest)
        return (carry + term, None)
    p_total, _ = lax.scan(add_p, jnp.zeros((HID_ALL, R), jnp.float32), jnp.arange(REPLICAS, dtype=jnp.int32))
    columns = []
    for column in range(R):
        vector = p_total[:, column]
        if columns:
            basis = jnp.stack(columns, 1)
            vector = vector - jnp.dot(basis, jnp.dot(basis.T, vector, precision=highest), precision=highest)
        vector = vector / jnp.sqrt(jnp.sum(vector * vector))
        columns.append(vector)
    p_hat = jnp.stack(columns, 1)

    def add_q(carry, index):
        proj = jnp.dot(grads[index].astype(jnp.float32), p_hat, precision=highest)
        term = lax.dot_general(acts[index].astype(jnp.float32), proj, contract, precision=highest)
        term = term + lax.dot_general(feedback[index].astype(jnp.float32), p_hat, contract, precision=highest)
        return (carry + term, None)
    q_factor, _ = lax.scan(add_q, jnp.zeros((D, R), jnp.float32), jnp.arange(REPLICAS, dtype=jnp.int32))
    approx = jnp.dot(p_hat, q_factor.T, precision=highest) / REPLICAS

    def renew(index):
        grad = lax.dot_general(grads[index], acts[index], contract, preferred_element_type=jnp.float32)
        merged = grad + feedback[index].astype(jnp.float32)
        return (merged - approx).astype(jnp.bfloat16)
    new_feedback = lax.map(renew, jnp.arange(REPLICAS, dtype=jnp.int32))
    return (q_factor, approx.astype(jnp.bfloat16), new_feedback)
```

```python
import functools

import jax
import jax.numpy as jnp
from jax import lax
from jax.experimental import pallas as pl
from jax.experimental.pallas import tpu as pltpu
from jax.sharding import PartitionSpec as P

MIB = 1 << 20
HIGHEST = lax.Precision.HIGHEST
NN = (((1,), (0,)), ((), ()))
NT = (((1,), (1,)), ((), ()))
TN = (((0,), (0,)), ((), ()))


def split2(x):
    hi = x.astype(jnp.bfloat16)
    lo = (x - hi.astype(jnp.float32)).astype(jnp.bfloat16)
    return hi, lo


def dot(a, b, dims):
    return lax.dot_general(a, b, dims, preferred_element_type=jnp.float32)


def grad_kernel(go_ref, tok_ref, fb_ref, q_ref, merged_ref, p_ref):
    width = tok_ref.shape[1]
    rank, rows = p_ref.shape
    step = pl.program_id(0)
    merged = dot(go_ref[...], tok_ref[...], NN) + fb_ref[...].astype(jnp.float32)
    merged_ref[:, pl.ds(pl.multiple_of(step * width, width), width)] = merged
    q2 = jnp.concatenate(split2(q_ref[...]), 0)
    m2 = jnp.concatenate(split2(merged), 0)
    part = dot(q2, m2, NT)
    part = part[:rank] + part[rank:]
    part = part[:, :rows] + part[:, rows:]

    @pl.when(step == 0)
    def _():
        p_ref[...] = part

    @pl.when(step > 0)
    def _():
        p_ref[...] += part


def z_kernel(index_ref, p_ref, merged_ref, z_ref, *, pieces, piece):
    rank, rows = p_ref.shape
    p = p_ref[...]
    hi, lo = split2(p)
    p2 = jnp.concatenate([jnp.concatenate([hi, hi], 1), jnp.concatenate([lo, lo], 1)], 0)
    for k in range(pieces):
        start = pl.multiple_of(index_ref[k] * piece, piece)
        m2 = jnp.concatenate(split2(merged_ref[:, pl.ds(start, piece)]), 0)
        part = dot(p2, m2, NN)
        z_ref[:, k * piece : (k + 1) * piece] = part[:rank] + part[rank:]
    gram = lax.dot_general(p, p, NT, precision=HIGHEST, preferred_element_type=jnp.float32)
    z_ref[:, pieces * piece :] = jnp.concatenate([gram, jnp.zeros((rank, 128 - rank), jnp.float32)], 1)


def factor_kernel(gram_ref, p_ref, a_ref, *, replicas):
    rank = gram_ref.shape[0]
    rows = p_ref.shape[1]
    lane = lax.broadcasted_iota(jnp.int32, (rank, 128), 1)
    sub = lax.broadcasted_iota(jnp.int32, (rank, 128), 0)
    work = jnp.where(lane < rank, gram_ref[...], jnp.where(lane == sub + rank, 1.0, 0.0))
    for j in range(rank):
        row = work[j : j + 1, :]
        col = work[:, j : j + 1]
        inv = 1.0 / jnp.sqrt(work[j : j + 1, j : j + 1])
        row = row * inv
        work = jnp.where(sub == j, row, jnp.where(sub > j, work - (col * inv) * row, work))
    inverse = work[:, rank : 2 * rank]
    p_hat = lax.dot_general(inverse, p_ref[...], NN, precision=HIGHEST, preferred_element_type=jnp.float32)
    a_ref[:rank, :] = inverse
    a_ref[rank:, :] = lax.dot_general(p_hat, inverse, TN, precision=HIGHEST, preferred_element_type=jnp.float32) / replicas


def finish_kernel(index_ref, a_ref, z_ref, merged_ref, *refs):
    q_ref, update_ref, feedback_ref = refs[-3:]
    rank = z_ref.shape[0]
    width = z_ref.shape[1]
    half = width // 2
    a = a_ref[...]
    a1, a2 = split2(a)
    a3 = (a - a1.astype(jnp.float32) - a2.astype(jnp.float32)).astype(jnp.bfloat16)
    a6 = jnp.concatenate([a1, a1, a2, a1, a2, a3], 1)
    step = pl.program_id(0)
    base = pl.multiple_of(index_ref[step] * width, width)
    flip = index_ref[pl.num_programs(0)]
    for h in range(2):
        z = z_ref[:, h * half : (h + 1) * half]
        z1, z2 = split2(z)
        z3 = (z - z1.astype(jnp.float32) - z2.astype(jnp.float32)).astype(jnp.bfloat16)
        z6 = jnp.concatenate([z1, z2, z1, z3, z2, z1], 0)
        out = dot(a6, z6, NN)
        place = pl.multiple_of((h ^ flip) * half, half)
        approx = out[rank:]
        q_ref[:, pl.ds(place, half)] = out[:rank]
        update_ref[:, pl.ds(place, half)] = approx.astype(jnp.bfloat16)
        merged = merged_ref[:, pl.ds(pl.multiple_of(base + place, half), half)]
        feedback_ref[:, pl.ds(place, half)] = (merged - approx).astype(jnp.bfloat16)


def grad_call(go, tokens, feedback, q, width=1024):
    rows, toks = go.shape
    d = tokens.shape[1]
    rank = q.shape[0]
    return pl.pallas_call(
        grad_kernel,
        grid=(d // width,),
        in_specs=[
            pl.BlockSpec((rows, toks), lambda j: (0, 0)),
            pl.BlockSpec((toks, width), lambda j: (0, j)),
            pl.BlockSpec((rows, width), lambda j: (0, j)),
            pl.BlockSpec((rank, width), lambda j: (0, j)),
        ],
        out_specs=[pl.BlockSpec(memory_space=pltpu.VMEM)] * 2,
        out_shape=[
            jax.ShapeDtypeStruct((rows, d), jnp.float32),
            jax.ShapeDtypeStruct((rank, rows), jnp.float32),
        ],
        compiler_params=pltpu.CompilerParams(vmem_limit_bytes=16 * MIB),
        name="grad_and_p",
    )(go, tokens, feedback, q)


def z_call(index, p, merged, pieces, piece, name):
    rank = p.shape[0]
    return pl.pallas_call(
        functools.partial(z_kernel, pieces=pieces, piece=piece),
        in_specs=[pl.BlockSpec(memory_space=pltpu.SMEM)] + [pl.BlockSpec(memory_space=pltpu.VMEM)] * 2,
        out_specs=pl.BlockSpec(memory_space=pltpu.VMEM),
        out_shape=jax.ShapeDtypeStruct((rank, pieces * piece + 128), jnp.float32),
        compiler_params=pltpu.CompilerParams(vmem_limit_bytes=16 * MIB),
        name=name,
    )(index, p, merged)


def factor_call(gram, p, replicas):
    rank, rows = p.shape
    return pl.pallas_call(
        functools.partial(factor_kernel, replicas=replicas),
        in_specs=[pl.BlockSpec(memory_space=pltpu.VMEM)] * 2,
        out_specs=pl.BlockSpec(memory_space=pltpu.VMEM),
        out_shape=jax.ShapeDtypeStruct((rank + rows, rank), jnp.float32),
        name="factor",
    )(gram, p)


def finish_call(index, a, z, merged, d, steps, earlier, name):
    rank, width = z.shape[0], z.shape[1] // steps
    rows = merged.shape[0]
    place = lambda j, index: (0, index[j])
    return pl.pallas_call(
        finish_kernel,
        grid_spec=pltpu.PrefetchScalarGridSpec(
            num_scalar_prefetch=1,
            grid=(steps,),
            in_specs=[
                pl.BlockSpec(a.shape, lambda j, index: (0, 0)),
                pl.BlockSpec((rank, width), lambda j, index: (0, j)),
                pl.BlockSpec(memory_space=pltpu.VMEM),
            ]
            + [pl.BlockSpec(memory_space=pl.ANY)] * len(earlier),
            out_specs=[
                pl.BlockSpec((rank, width), place),
                pl.BlockSpec((rows, width), place),
                pl.BlockSpec((rows, width), place),
            ],
        ),
        out_shape=[
            jax.ShapeDtypeStruct((rank, d), jnp.float32),
            jax.ShapeDtypeStruct((rows, d), jnp.bfloat16),
            jax.ShapeDtypeStruct((rows, d), jnp.bfloat16),
        ],
        input_output_aliases={4 + i: i for i in range(len(earlier))},
        compiler_params=pltpu.CompilerParams(vmem_limit_bytes=16 * MIB),
        name=name,
    )(index, a, z, merged, *earlier)


def solution(mesh):
    replicas, shards = mesh.shape["dp"], mesh.shape["tensor"]
    devices = replicas * shards
    side = 1 << ((replicas.bit_length() - 1) // 2)
    core, near_x, near_y, near_z = 1, shards, side * shards, 2
    cube = [near_x, near_y, near_z, near_x | near_y, near_x | near_z, near_y | near_z, near_x | near_y | near_z]
    order = [1, 2, 4, 3, 5, 6, 7]
    far_dp = [f * shards for f in (1 << b for b in range(replicas.bit_length() - 1)) if f not in (1, side)]
    far_tensor = [1 << b for b in range(2, shards.bit_length() - 1)]

    def flip(x, mask):
        return lax.ppermute(x, ("dp", "tensor"), [(i, i ^ mask) for i in range(devices)])

    def sum_dp(p):
        if replicas == 4:
            return (p + flip(p, near_x)) + (flip(p, near_y) + flip(p, near_x | near_y))
        for b in range(replicas.bit_length() - 1):
            p = p + flip(p, shards << b)
        return p

    def on_device(tokens, grad_out, feedback, q_prev):
        d = tokens.shape[1]
        half, piece = d // 2, d // 16
        dp, tensor = lax.axis_index("dp"), lax.axis_index("tensor")
        own = tensor % 2
        chip = dp % 2 + 2 * ((dp // side) % 2) + 4 * ((tensor // 2) % 2)
        ranks = jnp.arange(8, dtype=jnp.int32)
        mine, sibling = own * 8 + (chip ^ ranks), (1 - own) * 8 + (chip ^ ranks)

        merged, p = grad_call(grad_out.T, tokens, feedback[0], q_prev.T)
        p = sum_dp(p)
        other = z_call(sibling, p, merged, 8, piece, "z_sibling")
        z = z_call(mine, p, merged, 8, piece, "z_mine")
        z = z + flip(other, core)
        gram = z[:, half:]
        total = z[:, :piece]
        for k, mask in zip(order, cube):
            part = z[:, k * piece : (k + 1) * piece]
            if mask == near_z:
                part = flip(jnp.concatenate([part, gram], 1), mask)
                gram = gram + part[:, piece:]
                part = part[:, :piece]
            else:
                part = flip(part, mask)
            total = total + part
        for mask in far_dp:
            total = total + flip(total, mask)
        both = jnp.concatenate([total, gram], 1)
        for mask in far_tensor:
            both = both + flip(both, mask)
        total, gram = both[:, :piece], both[:, piece:]
        a = factor_call(gram, p, replicas)
        pieces = {0: total}
        for k, mask in zip(order, cube):
            pieces[k] = flip(total, mask)
        z_mine = jnp.concatenate([pieces[k] for k in range(8)], 1)
        z_other = flip(z_mine, core)
        pairs = jnp.arange(4, dtype=jnp.int32)
        swap = (chip % 2)[None]
        index = jnp.concatenate([own * 4 + (chip // 2 ^ pairs), swap])
        outs = finish_call(index, a, z_mine, merged, d, 4, (), "finish_mine")
        index = jnp.concatenate([(1 - own) * 4 + (chip // 2 ^ pairs), swap])
        q, update, new_feedback = finish_call(index, a, z_other, merged, d, 4, outs, "finish_sibling")
        return q.T, update, new_feedback[None]

    return jax.shard_map(
        on_device,
        mesh=mesh,
        in_specs=(P("dp", None), P("dp", "tensor"), P("dp", "tensor", None), P()),
        out_specs=(P(), P("tensor", None), P("dp", "tensor", None)),
        check_vma=False,
    )
```

```python
import functools

import jax
import jax.numpy as jnp
from jax import lax
from jax.experimental import pallas as pl
from jax.experimental.pallas import tpu as pltpu
from jax.sharding import PartitionSpec as P

MIB = 1 << 20
HIGHEST = lax.Precision.HIGHEST
NN = (((1,), (0,)), ((), ()))
NT = (((1,), (1,)), ((), ()))
TN = (((0,), (0,)), ((), ()))


def split2(x):
    hi = x.astype(jnp.bfloat16)
    lo = (x - hi.astype(jnp.float32)).astype(jnp.bfloat16)
    return hi, lo


def dot(a, b, dims):
    return lax.dot_general(a, b, dims, preferred_element_type=jnp.float32)


def in_hbm(x):
    return pltpu.with_memory_space_constraint(x, pltpu.HBM)


def grad_kernel(go_hbm, tok_hbm, fb_hbm, q_hbm, merged_ref, p_ref, go_v, tok_v, fb_v, q_v, sems, *, widths):
    rank, rows = p_ref.shape
    starts = [sum(widths[:k]) for k in range(len(widths))]
    copy_go = pltpu.make_async_copy(go_hbm, go_v, sems.at[0])
    copy_go.start()
    copies = []
    for k, (start, width) in enumerate(zip(starts, widths)):
        part = pl.ds(start, width)
        block = [
            pltpu.make_async_copy(whole.at[:, part], local.at[:, part], sems.at[1 + 3 * k + i])
            for i, (whole, local) in enumerate([(tok_hbm, tok_v), (fb_hbm, fb_v), (q_hbm, q_v)])
        ]
        for copy in block:
            copy.start()
        copies.append(block)
    copy_go.wait()
    go = go_v[...]
    total = None
    for k, (start, width) in enumerate(zip(starts, widths)):
        for copy in copies[k]:
            copy.wait()
        part = pl.ds(start, width)
        merged = dot(go, tok_v[:, part], NN) + fb_v[:, part].astype(jnp.float32)
        merged_ref[:, part] = merged
        q2 = jnp.concatenate(split2(q_v[:, part]), 0)
        m2 = jnp.concatenate(split2(merged), 0)
        term = dot(q2, m2, NT)
        total = term if total is None else total + term
    total = total[:rank] + total[rank:]
    p_ref[...] = total[:, :rows] + total[:, rows:]


def z_kernel(index_ref, p_ref, merged_ref, z_ref, *, pieces, piece):
    rank, rows = p_ref.shape
    p = p_ref[...]
    hi, lo = split2(p)
    p2 = jnp.concatenate([jnp.concatenate([hi, hi], 1), jnp.concatenate([lo, lo], 1)], 0)
    for k in range(pieces):
        start = pl.multiple_of(index_ref[k] * piece, piece)
        m2 = jnp.concatenate(split2(merged_ref[:, pl.ds(start, piece)]), 0)
        part = dot(p2, m2, NN)
        z_ref[:, k * piece : (k + 1) * piece] = part[:rank] + part[rank:]
    gram = lax.dot_general(p, p, NT, precision=HIGHEST, preferred_element_type=jnp.float32)
    z_ref[:, pieces * piece :] = jnp.concatenate([gram, jnp.zeros((rank, 128 - rank), jnp.float32)], 1)


def factor_kernel(gram_ref, p_ref, a_ref, *, replicas):
    rank = gram_ref.shape[0]
    lane = lax.broadcasted_iota(jnp.int32, (rank, 128), 1)
    sub = lax.broadcasted_iota(jnp.int32, (rank, 128), 0)
    work = jnp.where(lane < rank, gram_ref[...], jnp.where(lane == sub + rank, 1.0, 0.0))
    for j in range(rank - 1):
        col = jnp.broadcast_to(work[:, j : j + 1], (rank, 128))
        row = work[j : j + 1, :]
        scale = row / col[j : j + 1, :]
        work = work - jnp.where(sub > j, col, 0.0) * scale
    pivots = jnp.sum(jnp.where(lane == sub, work, 0.0), 1, keepdims=True)
    inverse = (work / jnp.sqrt(pivots))[:, rank : 2 * rank]
    p_hat = lax.dot_general(inverse, p_ref[...], NN, precision=HIGHEST, preferred_element_type=jnp.float32)
    approx = lax.dot_general(p_hat, inverse, TN, precision=HIGHEST, preferred_element_type=jnp.float32) / replicas
    hi, lo = split2(jnp.concatenate([inverse, approx], 0))
    a_ref[...] = jnp.concatenate([hi, hi, lo], 1)


def finish_kernel(*refs, inputs, earlier, piece):
    index_ref, a_ref, merged_ref = refs[:3]
    z_refs = refs[3 : 3 + inputs]
    q_hbm, update_hbm, feedback_hbm, q_v, update_v, feedback_v, sems = refs[3 + inputs + earlier :]
    rank = q_v.shape[0]
    a = a_ref[...]
    copies = []
    k = 0
    for z_ref in z_refs:
        for h in range(z_ref.shape[1] // piece):
            hi, lo = split2(z_ref[:, h * piece : (h + 1) * piece])
            out = dot(a, jnp.concatenate([hi, lo, hi], 0), NN)
            here = pl.ds(k * piece, piece)
            there = pl.ds(pl.multiple_of(index_ref[k] * piece, piece), piece)
            approx = out[rank:]
            q_v[:, here] = out[:rank]
            update_v[:, here] = approx.astype(jnp.bfloat16)
            feedback_v[:, here] = (merged_ref[:, there] - approx).astype(jnp.bfloat16)
            for i, (local, whole) in enumerate([(q_v, q_hbm), (update_v, update_hbm), (feedback_v, feedback_hbm)]):
                copy = pltpu.make_async_copy(local.at[:, here], whole.at[:, there], sems.at[3 * k + i])
                copy.start()
                copies.append(copy)
            k += 1
    for copy in copies:
        copy.wait()


def grad_call(go, tokens, feedback, q):
    rows, toks = go.shape
    d = tokens.shape[1]
    rank = q.shape[0]
    widths = [d // 4] * 3 + [d // 8] * 2
    return pl.pallas_call(
        functools.partial(grad_kernel, widths=widths),
        in_specs=[pl.BlockSpec(memory_space=pl.ANY)] * 4,
        out_specs=[pl.BlockSpec(memory_space=pltpu.VMEM)] * 2,
        out_shape=[
            jax.ShapeDtypeStruct((rows, d), jnp.float32),
            jax.ShapeDtypeStruct((rank, rows), jnp.float32),
        ],
        scratch_shapes=[
            pltpu.VMEM((rows, toks), go.dtype),
            pltpu.VMEM((toks, d), tokens.dtype),
            pltpu.VMEM((rows, d), feedback.dtype),
            pltpu.VMEM((rank, d), q.dtype),
            pltpu.SemaphoreType.DMA((1 + 3 * len(widths),)),
        ],
        compiler_params=pltpu.CompilerParams(vmem_limit_bytes=24 * MIB),
        name="grad_and_p",
    )(*[in_hbm(x) for x in (go, tokens, feedback, q)])


def z_call(index, p, merged, pieces, piece, name):
    rank, rows = p.shape
    return pl.pallas_call(
        functools.partial(z_kernel, pieces=pieces, piece=piece),
        in_specs=[pl.BlockSpec(memory_space=pltpu.SMEM)] + [pl.BlockSpec(memory_space=pltpu.VMEM)] * 2,
        out_specs=pl.BlockSpec(memory_space=pltpu.VMEM),
        out_shape=jax.ShapeDtypeStruct((rank, pieces * piece + 128), jnp.float32),
        compiler_params=pltpu.CompilerParams(vmem_limit_bytes=16 * MIB),
        cost_estimate=pl.CostEstimate(flops=8 * rank * rows * pieces * piece, bytes_accessed=2 * MIB, transcendentals=0),
        name=name,
    )(index, p, merged)


def factor_call(gram, p, replicas):
    rank, rows = p.shape
    return pl.pallas_call(
        functools.partial(factor_kernel, replicas=replicas),
        in_specs=[pl.BlockSpec(memory_space=pltpu.VMEM)] * 2,
        out_specs=pl.BlockSpec(memory_space=pltpu.VMEM),
        out_shape=jax.ShapeDtypeStruct((rank + rows, 3 * rank), jnp.bfloat16),
        compiler_params=pltpu.CompilerParams(vmem_limit_bytes=8 * MIB),
        cost_estimate=pl.CostEstimate(flops=10**9, bytes_accessed=8 * MIB, transcendentals=0),
        name="factor",
    )(gram, p)


def finish_call(index, a, merged, zs, d, piece, earlier, name):
    rank = zs[0].shape[0]
    rows = merged.shape[0]
    width = sum(z.shape[1] for z in zs)
    vmem, anywhere = pl.BlockSpec(memory_space=pltpu.VMEM), pl.BlockSpec(memory_space=pl.ANY)
    return pl.pallas_call(
        functools.partial(finish_kernel, inputs=len(zs), earlier=len(earlier), piece=piece),
        in_specs=[pl.BlockSpec(memory_space=pltpu.SMEM)] + [vmem] * (2 + len(zs)) + [anywhere] * len(earlier),
        out_specs=[pl.BlockSpec(memory_space=pltpu.HBM)] * 3,
        out_shape=[
            jax.ShapeDtypeStruct((rank, d), jnp.float32),
            jax.ShapeDtypeStruct((rows, d), jnp.bfloat16),
            jax.ShapeDtypeStruct((rows, d), jnp.bfloat16),
        ],
        scratch_shapes=[
            pltpu.VMEM((rank, width), jnp.float32),
            pltpu.VMEM((rows, width), jnp.bfloat16),
            pltpu.VMEM((rows, width), jnp.bfloat16),
            pltpu.SemaphoreType.DMA((3 * width // piece,)),
        ],
        input_output_aliases={3 + len(zs) + i: i for i in range(len(earlier))},
        compiler_params=pltpu.CompilerParams(vmem_limit_bytes=16 * MIB),
        cost_estimate=pl.CostEstimate(flops=10**8, bytes_accessed=4 * MIB, transcendentals=0),
        name=name,
    )(index, a, merged, *zs, *earlier)


def solution(mesh):
    replicas, shards = mesh.shape["dp"], mesh.shape["tensor"]
    devices = replicas * shards
    side = 1 << ((replicas.bit_length() - 1) // 2)
    core, near_x, near_y, near_z = 1, shards, side * shards, 2
    order = [0, 1, 2, 4, 3, 5, 6, 7]
    masks = [(near_x if r & 1 else 0) | (near_y if r & 2 else 0) | (near_z if r & 4 else 0) for r in order]
    far_dp = [f * shards for f in (1 << b for b in range(replicas.bit_length() - 1)) if f not in (1, side)]
    far_tensor = [1 << b for b in range(2, shards.bit_length() - 1)]

    def flip(x, mask):
        return lax.ppermute(x, ("dp", "tensor"), [(i, i ^ mask) for i in range(devices)])

    def sum_dp(p):
        if replicas == 4:
            return (p + flip(p, near_x)) + (flip(p, near_y) + flip(p, near_x | near_y))
        for b in range(replicas.bit_length() - 1):
            p = p + flip(p, shards << b)
        return p

    def on_device(tokens, grad_out, feedback, q_prev):
        d = tokens.shape[1]
        half, piece = d // 2, d // 16
        dp, tensor = lax.axis_index("dp"), lax.axis_index("tensor")
        own = tensor % 2
        chip = dp % 2 + 2 * ((dp // side) % 2) + 4 * ((tensor // 2) % 2)
        places = chip ^ jnp.array(order, jnp.int32)
        mine, sibling = own * 8 + places, (1 - own) * 8 + places

        merged, p = grad_call(grad_out.T, tokens, feedback[0], q_prev.T)
        p = sum_dp(p)
        other = z_call(sibling, p, merged, 8, piece, "z_sibling")
        z = z_call(mine, p, merged, 8, piece, "z_mine")
        z = z + flip(other, core)
        gram = z[:, half:]
        total = z[:, :piece]
        for k, mask in list(enumerate(masks))[1:]:
            part = z[:, k * piece : (k + 1) * piece]
            if mask == near_z:
                part = flip(jnp.concatenate([part, gram], 1), mask)
                gram = gram + part[:, piece:]
                part = part[:, :piece]
            else:
                part = flip(part, mask)
            total = total + part
        for mask in far_dp:
            total = total + flip(total, mask)
        both = jnp.concatenate([total, gram], 1)
        for mask in far_tensor:
            both = both + flip(both, mask)
        total, gram = both[:, :piece], both[:, piece:]
        a = factor_call(gram, p, replicas)
        pieces = [total] + [flip(total, mask) for mask in masks[1:]]
        first, a = lax.optimization_barrier((jnp.concatenate(pieces[:4], 1), a))
        others = [flip(first, core), flip(jnp.concatenate(pieces[4:], 1), core)]
        outs = finish_call(mine, a, merged, pieces, d, piece, (), "finish_mine")
        q, update, new_feedback = finish_call(sibling, a, merged, others, d, piece, outs, "finish_sibling")
        return q.T, update, new_feedback[None]

    return jax.shard_map(
        on_device,
        mesh=mesh,
        in_specs=(P("dp", None), P("dp", "tensor"), P("dp", "tensor", None), P()),
        out_specs=(P(), P("tensor", None), P("dp", "tensor", None)),
        check_vma=False,
    )
```

```python
import functools

import jax
import jax.numpy as jnp
from jax import lax
from jax.experimental import pallas as pl
from jax.experimental.pallas import tpu as pltpu
from jax.sharding import PartitionSpec as P

MIB = 1 << 20
HIGHEST = lax.Precision.HIGHEST
NN = (((1,), (0,)), ((), ()))
NT = (((1,), (1,)), ((), ()))
TN = (((0,), (0,)), ((), ()))


def split2(x):
    hi = x.astype(jnp.bfloat16)
    lo = (x - hi.astype(jnp.float32)).astype(jnp.bfloat16)
    return hi, lo


def dot(a, b, dims):
    return lax.dot_general(a, b, dims, preferred_element_type=jnp.float32)


def in_hbm(x):
    return pltpu.with_memory_space_constraint(x, pltpu.HBM)


def grad_kernel(go_hbm, tok_hbm, fb_hbm, q_hbm, merged_ref, p_ref, go_v, tok_v, fb_v, q_v, sems, *, widths):
    rank, rows = p_ref.shape
    starts = [sum(widths[:k]) for k in range(len(widths))]
    copy_go = pltpu.make_async_copy(go_hbm, go_v, sems.at[0])
    copy_go.start()
    copies = []
    for k, (start, width) in enumerate(zip(starts, widths)):
        part = pl.ds(start, width)
        block = [
            pltpu.make_async_copy(whole.at[:, part], local.at[:, part], sems.at[1 + 3 * k + i])
            for i, (whole, local) in enumerate([(tok_hbm, tok_v), (fb_hbm, fb_v), (q_hbm, q_v)])
        ]
        for copy in block:
            copy.start()
        copies.append(block)
    copy_go.wait()
    go = go_v[...]
    total = None
    for k, (start, width) in enumerate(zip(starts, widths)):
        for copy in copies[k]:
            copy.wait()
        part = pl.ds(start, width)
        merged = dot(go, tok_v[:, part], NN) + fb_v[:, part].astype(jnp.float32)
        merged_ref[:, part] = merged
        q2 = jnp.concatenate(split2(q_v[:, part]), 0)
        m2 = jnp.concatenate(split2(merged), 0)
        term = dot(q2, m2, NT)
        total = term if total is None else total + term
    total = total[:rank] + total[rank:]
    p_ref[...] = total[:, :rows] + total[:, rows:]


def place_of(k, sibling, side):
    dp, tensor = lax.axis_index("dp"), lax.axis_index("tensor")
    core = (tensor & 1) ^ sibling
    x, y, z = dp & 1, (dp // side) & 1, (tensor >> 1) & 1
    return core * 8 + (y ^ (k >> 2)) * 4 + (x ^ ((k >> 1) & 1)) * 2 + (z ^ (k & 1))


def z_kernel(p_ref, merged_ref, z_ref, *, pieces, piece, sibling, side):
    rank, rows = p_ref.shape
    p = p_ref[...]
    hi, lo = split2(p)
    p2 = jnp.concatenate([jnp.concatenate([hi, hi], 1), jnp.concatenate([lo, lo], 1)], 0)
    for k in range(pieces):
        start = pl.multiple_of(place_of(k, sibling, side) * piece, piece)
        m2 = jnp.concatenate(split2(merged_ref[:, pl.ds(start, piece)]), 0)
        part = dot(p2, m2, NN)
        z_ref[:, k * piece : (k + 1) * piece] = part[:rank] + part[rank:]
    gram = lax.dot_general(p, p, NT, precision=HIGHEST, preferred_element_type=jnp.float32)
    z_ref[:, pieces * piece :] = jnp.concatenate([gram, jnp.zeros((rank, 128 - rank), jnp.float32)], 1)


def factor_kernel(gram_ref, p_ref, a_ref, *, replicas):
    rank = gram_ref.shape[0]
    lane = lax.broadcasted_iota(jnp.int32, (rank, 128), 1)
    sub = lax.broadcasted_iota(jnp.int32, (rank, 128), 0)
    work = jnp.where(lane < rank, gram_ref[...], jnp.where(lane == sub + rank, 1.0, 0.0))
    for j in range(rank - 1):
        col = jnp.broadcast_to(work[:, j : j + 1], (rank, 128))
        row = work[j : j + 1, :]
        scale = row / col[j : j + 1, :]
        work = work - jnp.where(sub > j, col, 0.0) * scale
    pivots = jnp.sum(jnp.where(lane == sub, work, 0.0), 1, keepdims=True)
    inverse = (work / jnp.sqrt(pivots))[:, rank : 2 * rank]
    p_hat = lax.dot_general(inverse, p_ref[...], NN, precision=HIGHEST, preferred_element_type=jnp.float32)
    approx = lax.dot_general(p_hat, inverse, TN, precision=HIGHEST, preferred_element_type=jnp.float32) / replicas
    hi, lo = split2(jnp.concatenate([inverse, approx], 0))
    a_ref[...] = jnp.concatenate([hi, hi, lo], 1)


def finish_kernel(*refs, inputs, earlier, piece, sibling, side):
    a_ref, merged_ref = refs[:2]
    z_refs = refs[2 : 2 + inputs]
    q_hbm, update_hbm, feedback_hbm, q_v, update_v, feedback_v, sems = refs[2 + inputs + earlier :]
    rank = q_v.shape[0]
    a = a_ref[...]
    copies = []
    k = 0
    for z_ref in z_refs:
        for h in range(z_ref.shape[1] // piece):
            hi, lo = split2(z_ref[:, h * piece : (h + 1) * piece])
            out = dot(a, jnp.concatenate([hi, lo, hi], 0), NN)
            here = pl.ds(k * piece, piece)
            there = pl.ds(pl.multiple_of(place_of(k, sibling, side) * piece, piece), piece)
            approx = out[rank:]
            q_v[:, here] = out[:rank]
            update_v[:, here] = approx.astype(jnp.bfloat16)
            feedback_v[:, here] = (merged_ref[:, there] - approx).astype(jnp.bfloat16)
            for i, (local, whole) in enumerate([(q_v, q_hbm), (update_v, update_hbm), (feedback_v, feedback_hbm)]):
                copy = pltpu.make_async_copy(local.at[:, here], whole.at[:, there], sems.at[3 * k + i])
                copy.start()
                copies.append(copy)
            k += 1
    for copy in copies:
        copy.wait()


def grad_call(go, tokens, feedback, q):
    rows, toks = go.shape
    d = tokens.shape[1]
    rank = q.shape[0]
    widths = [d // 4] * 3 + [d // 8] * 2
    return pl.pallas_call(
        functools.partial(grad_kernel, widths=widths),
        in_specs=[pl.BlockSpec(memory_space=pl.ANY)] * 4,
        out_specs=[pl.BlockSpec(memory_space=pltpu.VMEM)] * 2,
        out_shape=[
            jax.ShapeDtypeStruct((rows, d), jnp.float32),
            jax.ShapeDtypeStruct((rank, rows), jnp.float32),
        ],
        scratch_shapes=[
            pltpu.VMEM((rows, toks), go.dtype),
            pltpu.VMEM((toks, d), tokens.dtype),
            pltpu.VMEM((rows, d), feedback.dtype),
            pltpu.VMEM((rank, d), q.dtype),
            pltpu.SemaphoreType.DMA((1 + 3 * len(widths),)),
        ],
        compiler_params=pltpu.CompilerParams(vmem_limit_bytes=24 * MIB),
        name="grad_and_p",
    )(*[in_hbm(x) for x in (go, tokens, feedback, q)])


def z_call(p, merged, pieces, piece, sibling, side, name):
    rank, rows = p.shape
    return pl.pallas_call(
        functools.partial(z_kernel, pieces=pieces, piece=piece, sibling=sibling, side=side),
        in_specs=[pl.BlockSpec(memory_space=pltpu.VMEM)] * 2,
        out_specs=pl.BlockSpec(memory_space=pltpu.VMEM),
        out_shape=jax.ShapeDtypeStruct((rank, pieces * piece + 128), jnp.float32),
        compiler_params=pltpu.CompilerParams(vmem_limit_bytes=16 * MIB),
        cost_estimate=pl.CostEstimate(flops=8 * rank * rows * pieces * piece, bytes_accessed=2 * MIB, transcendentals=0),
        name=name,
    )(p, merged)


def factor_call(gram, p, replicas):
    rank, rows = p.shape
    return pl.pallas_call(
        functools.partial(factor_kernel, replicas=replicas),
        in_specs=[pl.BlockSpec(memory_space=pltpu.VMEM)] * 2,
        out_specs=pl.BlockSpec(memory_space=pltpu.VMEM),
        out_shape=jax.ShapeDtypeStruct((rank + rows, 3 * rank), jnp.bfloat16),
        compiler_params=pltpu.CompilerParams(vmem_limit_bytes=8 * MIB),
        cost_estimate=pl.CostEstimate(flops=10**9, bytes_accessed=8 * MIB, transcendentals=0),
        name="factor",
    )(gram, p)


def finish_call(a, merged, zs, d, piece, earlier, sibling, side, name):
    rank = zs[0].shape[0]
    rows = merged.shape[0]
    width = sum(z.shape[1] for z in zs)
    vmem, anywhere = pl.BlockSpec(memory_space=pltpu.VMEM), pl.BlockSpec(memory_space=pl.ANY)
    return pl.pallas_call(
        functools.partial(finish_kernel, inputs=len(zs), earlier=len(earlier), piece=piece, sibling=sibling, side=side),
        in_specs=[vmem] * (2 + len(zs)) + [anywhere] * len(earlier),
        out_specs=[pl.BlockSpec(memory_space=pltpu.HBM)] * 3,
        out_shape=[
            jax.ShapeDtypeStruct((rank, d), jnp.float32),
            jax.ShapeDtypeStruct((rows, d), jnp.bfloat16),
            jax.ShapeDtypeStruct((rows, d), jnp.bfloat16),
        ],
        scratch_shapes=[
            pltpu.VMEM((rank, width), jnp.float32),
            pltpu.VMEM((rows, width), jnp.bfloat16),
            pltpu.VMEM((rows, width), jnp.bfloat16),
            pltpu.SemaphoreType.DMA((3 * width // piece,)),
        ],
        input_output_aliases={2 + len(zs) + i: i for i in range(len(earlier))},
        compiler_params=pltpu.CompilerParams(vmem_limit_bytes=16 * MIB),
        cost_estimate=pl.CostEstimate(flops=10**8, bytes_accessed=4 * MIB, transcendentals=0),
        name=name,
    )(a, merged, *zs, *earlier)


def solution(mesh):
    replicas, shards = mesh.shape["dp"], mesh.shape["tensor"]
    devices = replicas * shards
    side = 1 << ((replicas.bit_length() - 1) // 2)
    core, near_x, near_y, near_z = 1, shards, side * shards, 2
    plane = [0, near_x, near_y, near_x | near_y]
    far_dp = [f * shards for f in (1 << b for b in range(replicas.bit_length() - 1)) if f not in (1, side)]
    far_tensor = [1 << b for b in range(2, shards.bit_length() - 1)]

    def flip(x, mask):
        return lax.ppermute(x, ("dp", "tensor"), [(i, i ^ mask) for i in range(devices)])

    def sum_dp(p):
        if replicas == 4:
            return (p + flip(p, near_x)) + (flip(p, near_y) + flip(p, near_x | near_y))
        for b in range(replicas.bit_length() - 1):
            p = p + flip(p, shards << b)
        return p

    def on_device(tokens, grad_out, feedback, q_prev):
        d = tokens.shape[1]
        half, chunk, piece = d // 2, d // 8, d // 16
        merged, p = grad_call(grad_out.T, tokens, feedback[0], q_prev.T)
        p = sum_dp(p)
        other = z_call(p, merged, 8, piece, 1, side, "z_sibling")
        z = z_call(p, merged, 8, piece, 0, side, "z_mine")
        z = z + flip(other, core)
        gram = z[:, half:]
        slots = [z[:, k * chunk : (k + 1) * chunk] for k in range(4)]
        total = (slots[0] + flip(slots[1], plane[1])) + (flip(slots[2], plane[2]) + flip(slots[3], plane[3]))
        both = jnp.concatenate([total[:, :piece], gram], 1) + flip(jnp.concatenate([total[:, piece:], gram], 1), near_z)
        total, gram = both[:, :piece], both[:, piece:]
        for mask in far_dp:
            total = total + flip(total, mask)
        both = jnp.concatenate([total, gram], 1)
        for mask in far_tensor:
            both = both + flip(both, mask)
        total, gram = both[:, :piece], both[:, piece:]
        a = factor_call(gram, p, replicas)
        whole = jnp.concatenate([total, flip(total, near_z)], 1)
        whole, a = lax.optimization_barrier((whole, a))
        got = [whole] + [flip(whole, mask) for mask in plane[1:]]
        others = [flip(jnp.concatenate(got[:2], 1), core), flip(jnp.concatenate(got[2:], 1), core)]
        outs = finish_call(a, merged, got, d, piece, (), 0, side, "finish_mine")
        q, update, new_feedback = finish_call(a, merged, others, d, piece, outs, 1, side, "finish_sibling")
        return q.T, update, new_feedback[None]

    return jax.shard_map(
        on_device,
        mesh=mesh,
        in_specs=(P("dp", None), P("dp", "tensor"), P("dp", "tensor", None), P()),
        out_specs=(P(), P("tensor", None), P("dp", "tensor", None)),
        check_vma=False,
    )
```

```python
import functools

import jax
import jax.numpy as jnp
from jax import lax
from jax.experimental import pallas as pl
from jax.experimental.pallas import tpu as pltpu
from jax.sharding import PartitionSpec as P

MIB = 1 << 20
HIGHEST = lax.Precision.HIGHEST
NN = (((1,), (0,)), ((), ()))
NT = (((1,), (1,)), ((), ()))
TN = (((0,), (0,)), ((), ()))


def split2(x):
    hi = x.astype(jnp.bfloat16)
    lo = (x - hi.astype(jnp.float32)).astype(jnp.bfloat16)
    return hi, lo


def dot(a, b, dims):
    return lax.dot_general(a, b, dims, preferred_element_type=jnp.float32)


def in_hbm(x):
    return pltpu.with_memory_space_constraint(x, pltpu.HBM)


def grad_kernel(go_hbm, tok_hbm, fb_hbm, q_hbm, merged_ref, p_ref, go_v, tok_v, fb_v, q_v, qt_v, sems, *, width):
    rank, rows = p_ref.shape
    d = tok_hbm.shape[1]
    copy_go = pltpu.make_async_copy(go_hbm, go_v, sems.at[0])
    copy_q = pltpu.make_async_copy(q_hbm, q_v, sems.at[1])
    copy_go.start()
    copy_q.start()
    copies = []
    for k in range(d // width):
        part = pl.ds(k * width, width)
        block = [
            pltpu.make_async_copy(whole.at[:, part], local.at[:, part], sems.at[2 + 2 * k + i])
            for i, (whole, local) in enumerate([(fb_hbm, fb_v), (tok_hbm, tok_v)])
        ]
        for copy in block:
            copy.start()
        copies.append(block)
    copy_go.wait()
    go = go_v[...]
    copy_q.wait()
    for k in range(d // width):
        q2 = jnp.concatenate(split2(q_v[:, k * width : (k + 1) * width]), 0)
        qt_v[k * width : (k + 1) * width, :] = q2.T
    total = None
    for k in range(d // width):
        for copy in copies[k]:
            copy.wait()
        part = pl.ds(k * width, width)
        merged = dot(go, tok_v[:, part], NN) + fb_v[:, part].astype(jnp.float32)
        merged_ref[:, part] = merged
        term = dot(jnp.concatenate(split2(merged), 0), qt_v[part, :], NN)
        total = term if total is None else total + term
    total = total[:, :rank] + total[:, rank:]
    p_ref[...] = (total[:rows] + total[rows:]).T


def place_of(chunk, h, sibling, side):
    dp, tensor = lax.axis_index("dp"), lax.axis_index("tensor")
    core = (tensor & 1) ^ sibling
    x, y, z = dp & 1, (dp // side) & 1, (tensor >> 1) & 1
    return core * 8 + (y ^ (chunk >> 1)) * 4 + (x ^ (chunk & 1)) * 2 + (z ^ h)


def z_kernel(p_ref, merged_ref, z_ref, *, chunks, piece, sibling, side):
    rank, rows = p_ref.shape
    p = p_ref[...]
    hi, lo = split2(p)
    p2 = jnp.concatenate([jnp.concatenate([hi, hi], 1), jnp.concatenate([lo, lo], 1)], 0)
    for k in range(2 * len(chunks)):
        start = pl.multiple_of(place_of(chunks[k // 2], k % 2, sibling, side) * piece, piece)
        m2 = jnp.concatenate(split2(merged_ref[:, pl.ds(start, piece)]), 0)
        part = dot(p2, m2, NN)
        z_ref[:, k * piece : (k + 1) * piece] = part[:rank] + part[rank:]
    gram = lax.dot_general(p, p, NT, precision=HIGHEST, preferred_element_type=jnp.float32)
    z_ref[:, 2 * len(chunks) * piece :] = jnp.concatenate([gram, jnp.zeros((rank, 128 - rank), jnp.float32)], 1)


def factor_kernel(gram_ref, p_ref, a_ref, *, replicas):
    rank = gram_ref.shape[0]
    lane = lax.broadcasted_iota(jnp.int32, (rank, 128), 1)
    sub = lax.broadcasted_iota(jnp.int32, (rank, 128), 0)
    work = jnp.where(lane < rank, gram_ref[...], jnp.where(lane == sub + rank, 1.0, 0.0))
    for j in range(rank - 1):
        col = jnp.broadcast_to(work[:, j : j + 1], (rank, 128))
        row = work[j : j + 1, :]
        scale = row / col[j : j + 1, :]
        work = work - jnp.where(sub > j, col, 0.0) * scale
    pivots = jnp.sum(jnp.where(lane == sub, work, 0.0), 1, keepdims=True)
    inverse = (work / jnp.sqrt(pivots))[:, rank : 2 * rank]
    p_hat = lax.dot_general(inverse, p_ref[...], NN, precision=HIGHEST, preferred_element_type=jnp.float32)
    approx = lax.dot_general(p_hat, inverse, TN, precision=HIGHEST, preferred_element_type=jnp.float32) / replicas
    hi, lo = split2(jnp.concatenate([inverse, approx], 0))
    a_ref[...] = jnp.concatenate([hi, hi, lo], 1)


def finish_kernel(*refs, parts, earlier, piece, side):
    a_ref, merged_ref = refs[:2]
    z_refs = refs[2 : 2 + len(parts)]
    q_hbm, update_hbm, feedback_hbm, q_v, update_v, feedback_v, sems = refs[2 + len(parts) + earlier :]
    rank = q_v.shape[0]
    a = a_ref[...]
    copies = []
    k = 0
    for z_ref, (chunks, sibling) in zip(z_refs, parts):
        for h in range(2 * len(chunks)):
            hi, lo = split2(z_ref[:, h * piece : (h + 1) * piece])
            out = dot(a, jnp.concatenate([hi, lo, hi], 0), NN)
            here = pl.ds(k * piece, piece)
            there = pl.ds(pl.multiple_of(place_of(chunks[h // 2], h % 2, sibling, side) * piece, piece), piece)
            approx = out[rank:]
            q_v[:, here] = out[:rank]
            update_v[:, here] = approx.astype(jnp.bfloat16)
            feedback_v[:, here] = (merged_ref[:, there] - approx).astype(jnp.bfloat16)
            for i, (local, whole) in enumerate([(q_v, q_hbm), (update_v, update_hbm), (feedback_v, feedback_hbm)]):
                copy = pltpu.make_async_copy(local.at[:, here], whole.at[:, there], sems.at[3 * k + i])
                copy.start()
                copies.append(copy)
            k += 1
    for copy in copies:
        copy.wait()


def grad_call(go, tokens, feedback, q):
    rows, toks = go.shape
    d = tokens.shape[1]
    rank = q.shape[0]
    width = d // 4
    return pl.pallas_call(
        functools.partial(grad_kernel, width=width),
        in_specs=[pl.BlockSpec(memory_space=pl.ANY)] * 4,
        out_specs=[pl.BlockSpec(memory_space=pltpu.VMEM)] * 2,
        out_shape=[
            jax.ShapeDtypeStruct((rows, d), jnp.float32),
            jax.ShapeDtypeStruct((rank, rows), jnp.float32),
        ],
        scratch_shapes=[
            pltpu.VMEM((rows, toks), go.dtype),
            pltpu.VMEM((toks, d), tokens.dtype),
            pltpu.VMEM((rows, d), feedback.dtype),
            pltpu.VMEM((rank, d), q.dtype),
            pltpu.VMEM((d, 2 * rank), jnp.bfloat16),
            pltpu.SemaphoreType.DMA((2 + 2 * d // width,)),
        ],
        compiler_params=pltpu.CompilerParams(vmem_limit_bytes=24 * MIB),
        name="grad_and_p",
    )(*[in_hbm(x) for x in (go, tokens, feedback, q)])


def z_call(p, merged, chunks, piece, sibling, side, name):
    rank, rows = p.shape
    width = 2 * len(chunks) * piece
    return pl.pallas_call(
        functools.partial(z_kernel, chunks=chunks, piece=piece, sibling=sibling, side=side),
        in_specs=[pl.BlockSpec(memory_space=pltpu.VMEM)] * 2,
        out_specs=pl.BlockSpec(memory_space=pltpu.VMEM),
        out_shape=jax.ShapeDtypeStruct((rank, width + 128), jnp.float32),
        compiler_params=pltpu.CompilerParams(vmem_limit_bytes=16 * MIB),
        cost_estimate=pl.CostEstimate(flops=8 * rank * rows * width, bytes_accessed=2 * MIB, transcendentals=0),
        name=name,
    )(p, merged)


def factor_call(gram, p, replicas):
    rank, rows = p.shape
    return pl.pallas_call(
        functools.partial(factor_kernel, replicas=replicas),
        in_specs=[pl.BlockSpec(memory_space=pltpu.VMEM)] * 2,
        out_specs=pl.BlockSpec(memory_space=pltpu.VMEM),
        out_shape=jax.ShapeDtypeStruct((rank + rows, 3 * rank), jnp.bfloat16),
        compiler_params=pltpu.CompilerParams(vmem_limit_bytes=8 * MIB),
        cost_estimate=pl.CostEstimate(flops=10**9, bytes_accessed=8 * MIB, transcendentals=0),
        name="factor",
    )(gram, p)


def finish_call(a, merged, parts, d, piece, earlier, side, name):
    zs = [z for z, _, _ in parts]
    rank = zs[0].shape[0]
    rows = merged.shape[0]
    width = sum(z.shape[1] for z in zs)
    vmem, anywhere = pl.BlockSpec(memory_space=pltpu.VMEM), pl.BlockSpec(memory_space=pl.ANY)
    return pl.pallas_call(
        functools.partial(
            finish_kernel,
            parts=[(chunks, sibling) for _, chunks, sibling in parts],
            earlier=len(earlier),
            piece=piece,
            side=side,
        ),
        in_specs=[vmem] * (2 + len(zs)) + [anywhere] * len(earlier),
        out_specs=[pl.BlockSpec(memory_space=pltpu.HBM)] * 3,
        out_shape=[
            jax.ShapeDtypeStruct((rank, d), jnp.float32),
            jax.ShapeDtypeStruct((rows, d), jnp.bfloat16),
            jax.ShapeDtypeStruct((rows, d), jnp.bfloat16),
        ],
        scratch_shapes=[
            pltpu.VMEM((rank, width), jnp.float32),
            pltpu.VMEM((rows, width), jnp.bfloat16),
            pltpu.VMEM((rows, width), jnp.bfloat16),
            pltpu.SemaphoreType.DMA((3 * width // piece,)),
        ],
        input_output_aliases={2 + len(zs) + i: i for i in range(len(earlier))},
        compiler_params=pltpu.CompilerParams(vmem_limit_bytes=16 * MIB),
        cost_estimate=pl.CostEstimate(flops=10**8, bytes_accessed=4 * MIB, transcendentals=0),
        name=name,
    )(a, merged, *zs, *earlier)


def solution(mesh):
    replicas, shards = mesh.shape["dp"], mesh.shape["tensor"]
    devices = replicas * shards
    side = 1 << ((replicas.bit_length() - 1) // 2)
    core, near_x, near_y, near_z = 1, shards, side * shards, 2
    plane = [0, near_x, near_y, near_x | near_y]
    far_dp = [f * shards for f in (1 << b for b in range(replicas.bit_length() - 1)) if f not in (1, side)]
    far_tensor = [1 << b for b in range(2, shards.bit_length() - 1)]

    def flip(x, mask):
        return lax.ppermute(x, ("dp", "tensor"), [(i, i ^ mask) for i in range(devices)])

    def sum_dp(p):
        if replicas == 4:
            return (p + flip(p, near_x)) + (flip(p, near_y) + flip(p, near_x | near_y))
        for b in range(replicas.bit_length() - 1):
            p = p + flip(p, shards << b)
        return p

    def on_device(tokens, grad_out, feedback, q_prev):
        d = tokens.shape[1]
        chunk, piece = d // 8, d // 16
        merged, p = grad_call(grad_out.T, tokens, feedback[0], q_prev.T)
        p = sum_dp(p)
        chunks = (0, 3, 2, 1)
        other = flip(z_call(p, merged, chunks, piece, 1, side, "z_sibling"), core)
        z = z_call(p, merged, chunks, piece, 0, side, "z_mine") + other
        part = {c: z[:, k * chunk : (k + 1) * chunk] for k, c in enumerate(chunks)}
        gram = z[:, 4 * chunk :]
        total = (part[0] + flip(part[3], plane[3])) + (flip(part[2], plane[2]) + flip(part[1], plane[1]))
        both = jnp.concatenate([total[:, :piece], gram], 1) + flip(jnp.concatenate([total[:, piece:], gram], 1), near_z)
        total, gram = both[:, :piece], both[:, piece:]
        for mask in far_dp:
            total = total + flip(total, mask)
        both = jnp.concatenate([total, gram], 1)
        for mask in far_tensor:
            both = both + flip(both, mask)
        total, gram = both[:, :piece], both[:, piece:]
        a = factor_call(gram, p, replicas)
        whole = jnp.concatenate([total, flip(total, near_z)], 1)
        whole, a = lax.optimization_barrier((whole, a))
        got = {0: whole}
        for k in (3, 2, 1):
            got[k] = flip(whole, plane[k])
        outs = finish_call(a, merged, [(got[0], (0,), 0), (got[3], (3,), 0)], d, piece, (), side, "finish_first")
        first = flip(jnp.concatenate([got[0], got[3]], 1), core)
        second, outs = lax.optimization_barrier((jnp.concatenate([got[2], got[1]], 1), outs))
        second = flip(second, core)
        outs = finish_call(a, merged, [(got[2], (2,), 0), (got[1], (1,), 0)], d, piece, outs, side, "finish_second")
        q, update, new_feedback = finish_call(a, merged, [(first, (0, 3), 1), (second, (2, 1), 1)], d, piece, outs, side, "finish_third")
        return q.T, update, new_feedback[None]

    return jax.shard_map(
        on_device,
        mesh=mesh,
        in_specs=(P("dp", None), P("dp", "tensor"), P("dp", "tensor", None), P()),
        out_specs=(P(), P("tensor", None), P("dp", "tensor", None)),
        check_vma=False,
    )
```

```python
import functools

import jax
import jax.numpy as jnp
from jax import lax
from jax.experimental import pallas as pl
from jax.experimental.pallas import tpu as pltpu
from jax.sharding import PartitionSpec as P

MIB = 1 << 20
HIGHEST = lax.Precision.HIGHEST
NN = (((1,), (0,)), ((), ()))
NT = (((1,), (1,)), ((), ()))
TN = (((0,), (0,)), ((), ()))


def split2(x):
    hi = x.astype(jnp.bfloat16)
    lo = (x - hi.astype(jnp.float32)).astype(jnp.bfloat16)
    return hi, lo


def dot(a, b, dims):
    return lax.dot_general(a, b, dims, preferred_element_type=jnp.float32)


def in_hbm(x):
    return pltpu.with_memory_space_constraint(x, pltpu.HBM)


def grad_kernel(go_hbm, tok_hbm, fb_hbm, q_hbm, own_ref, other_ref, p_ref, go_v, tok_v, fb_v, q_v, qt_v, sems, *, blocks):
    rank, rows = p_ref.shape
    d = tok_hbm.shape[1]
    width = d // blocks
    core = lax.axis_index("tensor") & 1
    copy_go = pltpu.make_async_copy(go_hbm, go_v, sems.at[0])
    copy_go.start()
    copies_q = []
    for k in range(2):
        there = pl.ds(pl.multiple_of((core ^ k) * (d // 2), d // 2), d // 2)
        copies_q.append(pltpu.make_async_copy(q_hbm.at[:, there], q_v.at[:, pl.ds(k * (d // 2), d // 2)], sems.at[1 + k]))
        copies_q[k].start()
    copies = []
    for k in range(blocks):
        start = (core ^ (2 * k // blocks)) * (d // 2) + k % (blocks // 2) * width
        there = pl.ds(pl.multiple_of(start, width), width)
        block = [
            pltpu.make_async_copy(whole.at[:, there], local.at[:, pl.ds(k * width, width)], sems.at[3 + 2 * k + i])
            for i, (whole, local) in enumerate([(fb_hbm, fb_v), (tok_hbm, tok_v)])
        ]
        for copy in block:
            copy.start()
        copies.append(block)
    copy_go.wait()
    go = go_v[...]
    for copy in copies_q:
        copy.wait()
    for k in range(blocks):
        q2 = jnp.concatenate(split2(q_v[:, k * width : (k + 1) * width]), 0)
        qt_v[k * width : (k + 1) * width, :] = q2.T
    total = None
    for k in range(blocks):
        for copy in copies[k]:
            copy.wait()
        part = pl.ds(k * width, width)
        merged = dot(go, tok_v[:, part], NN) + fb_v[:, part].astype(jnp.float32)
        half_ref = own_ref if 2 * k < blocks else other_ref
        half_ref[:, pl.ds(k % (blocks // 2) * width, width)] = merged
        term = dot(jnp.concatenate(split2(merged), 0), qt_v[part, :], NN)
        total = term if total is None else total + term
    total = total[:, :rank] + total[:, rank:]
    p_ref[...] = (total[:rows] + total[rows:]).T


def place_of(chunk, h, side):
    dp, tensor = lax.axis_index("dp"), lax.axis_index("tensor")
    x, y, z = dp & 1, (dp // side) & 1, (tensor >> 1) & 1
    return (y ^ (chunk >> 1)) * 4 + (x ^ (chunk & 1)) * 2 + (z ^ h)


def z_kernel(p_ref, merged_ref, *refs, chunks, piece, side):
    z_ref = refs[-1]
    rank, rows = p_ref.shape
    p = p_ref[...]
    hi, lo = split2(p)
    p2 = jnp.concatenate([jnp.concatenate([hi, hi], 1), jnp.concatenate([lo, lo], 1)], 0)

    def put(start, width, value):
        z_ref[:, start : start + width] = value + refs[0][:, start : start + width] if len(refs) > 1 else value

    for k in range(2 * len(chunks)):
        start = pl.multiple_of(place_of(chunks[k // 2], k % 2, side) * piece, piece)
        m2 = jnp.concatenate(split2(merged_ref[:, pl.ds(start, piece)]), 0)
        part = dot(p2, m2, NN)
        put(k * piece, piece, part[:rank] + part[rank:])
    gram = lax.dot_general(p, p, NT, precision=HIGHEST, preferred_element_type=jnp.float32)
    put(2 * len(chunks) * piece, 128, jnp.concatenate([gram, jnp.zeros((rank, 128 - rank), jnp.float32)], 1))


def factor_kernel(gram_ref, p_ref, a_ref, *, replicas):
    rank = gram_ref.shape[0]
    lane = lax.broadcasted_iota(jnp.int32, (rank, 128), 1)
    sub = lax.broadcasted_iota(jnp.int32, (rank, 128), 0)
    work = jnp.where(lane < rank, gram_ref[...], jnp.where(lane == sub + rank, 1.0, 0.0))
    for j in range(rank - 1):
        col = jnp.broadcast_to(work[:, j : j + 1], (rank, 128))
        row = work[j : j + 1, :]
        scale = row / col[j : j + 1, :]
        work = work - jnp.where(sub > j, col, 0.0) * scale
    pivots = jnp.sum(jnp.where(lane == sub, work, 0.0), 1, keepdims=True)
    inverse = (work / jnp.sqrt(pivots))[:, rank : 2 * rank]
    p_hat = lax.dot_general(inverse, p_ref[...], NN, precision=HIGHEST, preferred_element_type=jnp.float32)
    approx = lax.dot_general(p_hat, inverse, TN, precision=HIGHEST, preferred_element_type=jnp.float32) / replicas
    hi, lo = split2(jnp.concatenate([inverse, approx], 0))
    a_ref[...] = jnp.concatenate([hi, hi, lo], 1)


def finish_kernel(*refs, parts, earlier, piece, side):
    a_ref, own_ref, other_ref = refs[:3]
    z_refs = refs[3 : 3 + len(parts)]
    q_hbm, update_hbm, feedback_hbm, q_v, update_v, feedback_v, sems = refs[3 + len(parts) + earlier :]
    half = q_hbm.shape[1] // 2
    rank = q_v.shape[0]
    a = a_ref[...]
    copies = []
    k = 0
    for z_ref, (chunks, sibling) in zip(z_refs, parts):
        for h in range(2 * len(chunks)):
            hi, lo = split2(z_ref[:, h * piece : (h + 1) * piece])
            out = dot(a, jnp.concatenate([hi, lo, hi], 0), NN)
            here = pl.ds(k * piece, piece)
            place = place_of(chunks[h // 2], h % 2, side) * piece
            there = pl.ds(pl.multiple_of(((lax.axis_index("tensor") & 1) ^ sibling) * half + place, piece), piece)
            merged_ref = other_ref if sibling else own_ref
            approx = out[rank:]
            q_v[:, here] = out[:rank]
            update_v[:, here] = approx.astype(jnp.bfloat16)
            feedback_v[:, here] = (merged_ref[:, pl.ds(pl.multiple_of(place, piece), piece)] - approx).astype(jnp.bfloat16)
            for i, (local, whole) in enumerate([(q_v, q_hbm), (update_v, update_hbm), (feedback_v, feedback_hbm)]):
                copy = pltpu.make_async_copy(local.at[:, here], whole.at[:, there], sems.at[3 * k + i])
                copy.start()
                copies.append(copy)
            k += 1
    for copy in copies:
        copy.wait()


def grad_call(go, tokens, feedback, q, blocks=4):
    rows, toks = go.shape
    d = tokens.shape[1]
    rank = q.shape[0]
    return pl.pallas_call(
        functools.partial(grad_kernel, blocks=blocks),
        in_specs=[pl.BlockSpec(memory_space=pl.ANY)] * 4,
        out_specs=[pl.BlockSpec(memory_space=pltpu.VMEM)] * 3,
        out_shape=[
            jax.ShapeDtypeStruct((rows, d // 2), jnp.float32),
            jax.ShapeDtypeStruct((rows, d // 2), jnp.float32),
            jax.ShapeDtypeStruct((rank, rows), jnp.float32),
        ],
        scratch_shapes=[
            pltpu.VMEM((rows, toks), go.dtype),
            pltpu.VMEM((toks, d), tokens.dtype),
            pltpu.VMEM((rows, d), feedback.dtype),
            pltpu.VMEM((rank, d), q.dtype),
            pltpu.VMEM((d, 2 * rank), jnp.bfloat16),
            pltpu.SemaphoreType.DMA((3 + 2 * blocks,)),
        ],
        compiler_params=pltpu.CompilerParams(vmem_limit_bytes=24 * MIB),
        name="grad_and_p",
    )(*[in_hbm(x) for x in (go, tokens, feedback, q)])


def z_call(p, merged, chunks, piece, earlier, side, name):
    rank, rows = p.shape
    width = 2 * len(chunks) * piece
    return pl.pallas_call(
        functools.partial(z_kernel, chunks=chunks, piece=piece, side=side),
        in_specs=[pl.BlockSpec(memory_space=pltpu.VMEM)] * (2 + len(earlier)),
        out_specs=pl.BlockSpec(memory_space=pltpu.VMEM),
        out_shape=jax.ShapeDtypeStruct((rank, width + 128), jnp.float32),
        compiler_params=pltpu.CompilerParams(vmem_limit_bytes=16 * MIB),
        cost_estimate=pl.CostEstimate(flops=8 * rank * rows * width, bytes_accessed=2 * MIB, transcendentals=0),
        name=name,
    )(p, merged, *earlier)


def factor_call(gram, p, replicas):
    rank, rows = p.shape
    return pl.pallas_call(
        functools.partial(factor_kernel, replicas=replicas),
        in_specs=[pl.BlockSpec(memory_space=pltpu.VMEM)] * 2,
        out_specs=pl.BlockSpec(memory_space=pltpu.VMEM),
        out_shape=jax.ShapeDtypeStruct((rank + rows, 3 * rank), jnp.bfloat16),
        compiler_params=pltpu.CompilerParams(vmem_limit_bytes=8 * MIB),
        cost_estimate=pl.CostEstimate(flops=10**9, bytes_accessed=8 * MIB, transcendentals=0),
        name="factor",
    )(gram, p)


def finish_call(a, own, other, parts, d, piece, earlier, side, name):
    zs = [z for z, _, _ in parts]
    rank = zs[0].shape[0]
    rows = own.shape[0]
    width = sum(z.shape[1] for z in zs)
    vmem, anywhere = pl.BlockSpec(memory_space=pltpu.VMEM), pl.BlockSpec(memory_space=pl.ANY)
    return pl.pallas_call(
        functools.partial(
            finish_kernel,
            parts=[(chunks, sibling) for _, chunks, sibling in parts],
            earlier=len(earlier),
            piece=piece,
            side=side,
        ),
        in_specs=[vmem] * (3 + len(zs)) + [anywhere] * len(earlier),
        out_specs=[pl.BlockSpec(memory_space=pltpu.HBM)] * 3,
        out_shape=[
            jax.ShapeDtypeStruct((rank, d), jnp.float32),
            jax.ShapeDtypeStruct((rows, d), jnp.bfloat16),
            jax.ShapeDtypeStruct((rows, d), jnp.bfloat16),
        ],
        scratch_shapes=[
            pltpu.VMEM((rank, width), jnp.float32),
            pltpu.VMEM((rows, width), jnp.bfloat16),
            pltpu.VMEM((rows, width), jnp.bfloat16),
            pltpu.SemaphoreType.DMA((3 * width // piece,)),
        ],
        input_output_aliases={3 + len(zs) + i: i for i in range(len(earlier))},
        compiler_params=pltpu.CompilerParams(vmem_limit_bytes=16 * MIB),
        cost_estimate=pl.CostEstimate(flops=10**8, bytes_accessed=4 * MIB, transcendentals=0),
        name=name,
    )(a, own, other, *zs, *earlier)


def solution(mesh):
    replicas, shards = mesh.shape["dp"], mesh.shape["tensor"]
    devices = replicas * shards
    side = 1 << ((replicas.bit_length() - 1) // 2)
    core, near_x, near_y, near_z = 1, shards, side * shards, 2
    plane = [0, near_x, near_y, near_x | near_y]
    far_dp = [f * shards for f in (1 << b for b in range(replicas.bit_length() - 1)) if f not in (1, side)]
    far_tensor = [1 << b for b in range(2, shards.bit_length() - 1)]

    def flip(x, mask):
        return lax.ppermute(x, ("dp", "tensor"), [(i, i ^ mask) for i in range(devices)])

    def sum_dp(p):
        if replicas == 4:
            return (p + flip(p, near_x)) + (flip(p, near_y) + flip(p, near_x | near_y))
        for b in range(replicas.bit_length() - 1):
            p = p + flip(p, shards << b)
        return p

    def on_device(tokens, grad_out, feedback, q_prev):
        d = tokens.shape[1]
        chunk, piece = d // 8, d // 16
        own, other, p = grad_call(grad_out.T, tokens, feedback[0], q_prev.T)
        siblings = flip(other, core)
        p = sum_dp(p)
        chunks = (0, 3, 2, 1)
        z = z_call(p, own, chunks, piece, (), side, "z_own_rows")
        z = z_call(flip(p, core), siblings, chunks, piece, (z,), side, "z_sibling_rows")
        part = {c: z[:, k * chunk : (k + 1) * chunk] for k, c in enumerate(chunks)}
        gram = z[:, 4 * chunk :]
        total = (part[0] + flip(part[3], plane[3])) + (flip(part[2], plane[2]) + flip(part[1], plane[1]))
        both = jnp.concatenate([total[:, :piece], gram], 1) + flip(jnp.concatenate([total[:, piece:], gram], 1), near_z)
        total, gram = both[:, :piece], both[:, piece:]
        for mask in far_dp:
            total = total + flip(total, mask)
        both = jnp.concatenate([total, gram], 1)
        for mask in far_tensor:
            both = both + flip(both, mask)
        total, gram = both[:, :piece], both[:, piece:]
        a = factor_call(gram, p, replicas)
        whole = jnp.concatenate([total, flip(total, near_z)], 1)
        whole, a = lax.optimization_barrier((whole, a))
        got = {0: whole}
        for k in (3, 2, 1):
            got[k] = flip(whole, plane[k])
        outs = finish_call(a, own, other, [(got[0], (0,), 0), (got[3], (3,), 0)], d, piece, (), side, "finish_first")
        first = flip(jnp.concatenate([got[0], got[3]], 1), core)
        second, outs = lax.optimization_barrier((jnp.concatenate([got[2], got[1]], 1), outs))
        second = flip(second, core)
        outs = finish_call(a, own, other, [(got[2], (2,), 0), (got[1], (1,), 0)], d, piece, outs, side, "finish_second")
        q, update, new_feedback = finish_call(a, own, other, [(first, (0, 3), 1), (second, (2, 1), 1)], d, piece, outs, side, "finish_third")
        return q.T, update, new_feedback[None]

    return jax.shard_map(
        on_device,
        mesh=mesh,
        in_specs=(P("dp", None), P("dp", "tensor"), P("dp", "tensor", None), P()),
        out_specs=(P(), P("tensor", None), P("dp", "tensor", None)),
        check_vma=False,
    )
```

```python
import functools

import jax
import jax.numpy as jnp
from jax import lax
from jax.experimental import pallas as pl
from jax.experimental.pallas import tpu as pltpu
from jax.sharding import PartitionSpec as P

MIB = 1 << 20
HIGHEST = lax.Precision.HIGHEST
NN = (((1,), (0,)), ((), ()))
NT = (((1,), (1,)), ((), ()))
TN = (((0,), (0,)), ((), ()))


def split2(x):
    hi = x.astype(jnp.bfloat16)
    lo = (x - hi.astype(jnp.float32)).astype(jnp.bfloat16)
    return hi, lo


def dot(a, b, dims):
    return lax.dot_general(a, b, dims, preferred_element_type=jnp.float32)


def pack(x):
    parts, rows = 128 // x.shape[1], x.shape[0] * x.shape[1] // 128
    return jnp.concatenate([x[i * rows : (i + 1) * rows] for i in range(parts)], 1)


def unpack(x, rank):
    return jnp.concatenate([x[:, i * rank : (i + 1) * rank] for i in range(128 // rank)], 0)


def stack(x):
    return jnp.concatenate([x[:, i : i + 128] for i in range(0, x.shape[1], 128)], 0)


def unstack(x, rank):
    return jnp.concatenate([x[i : i + rank] for i in range(0, x.shape[0], rank)], 1)


def in_hbm(x):
    return pltpu.with_memory_space_constraint(x, pltpu.HBM)


def grad_kernel(go_hbm, tok_hbm, fb_hbm, q_hbm, own_ref, other_ref, p_ref, go_v, tok_v, fb_v, q_v, qt_v, sems, *, blocks):
    rank, rows = p_ref.shape
    d = tok_hbm.shape[1]
    width = d // blocks
    core = lax.axis_index("tensor") & 1
    copy_go = pltpu.make_async_copy(go_hbm, go_v, sems.at[0])
    copy_go.start()
    copies_q = []
    for k in range(2):
        there = pl.ds(pl.multiple_of((core ^ k) * (d // 2), d // 2), d // 2)
        copies_q.append(pltpu.make_async_copy(q_hbm.at[:, there], q_v.at[:, pl.ds(k * (d // 2), d // 2)], sems.at[1 + k]))
        copies_q[k].start()
    copies = []
    for k in range(blocks):
        start = (core ^ (2 * k // blocks)) * (d // 2) + k % (blocks // 2) * width
        there = pl.ds(pl.multiple_of(start, width), width)
        block = [
            pltpu.make_async_copy(whole.at[:, there], local.at[:, pl.ds(k * width, width)], sems.at[3 + 2 * k + i])
            for i, (whole, local) in enumerate([(fb_hbm, fb_v), (tok_hbm, tok_v)])
        ]
        for copy in block:
            copy.start()
        copies.append(block)
    copy_go.wait()
    go = go_v[...]
    for copy in copies_q:
        copy.wait()
    for k in range(blocks):
        q2 = jnp.concatenate(split2(q_v[:, k * width : (k + 1) * width]), 0)
        qt_v[k * width : (k + 1) * width, :] = q2.T
    total = None
    for k in range(blocks):
        for copy in copies[k]:
            copy.wait()
        part = pl.ds(k * width, width)
        merged = dot(go, tok_v[:, part], NN) + fb_v[:, part].astype(jnp.float32)
        half_ref = own_ref if 2 * k < blocks else other_ref
        half_ref[:, pl.ds(k % (blocks // 2) * width, width)] = merged
        term = dot(jnp.concatenate(split2(merged), 0), qt_v[part, :], NN)
        total = term if total is None else total + term
    total = total[:, :rank] + total[:, rank:]
    p_ref[...] = (total[:rows] + total[rows:]).T


def place_of(chunk, h, side):
    dp, tensor = lax.axis_index("dp"), lax.axis_index("tensor")
    x, y, z = dp & 1, (dp // side) & 1, (tensor >> 1) & 1
    return (y ^ (chunk >> 1)) * 4 + (x ^ (chunk & 1)) * 2 + (z ^ h)


def z_kernel(p_ref, merged_ref, *refs, chunks, piece, side):
    z_ref = refs[-1]
    rank, rows = p_ref.shape
    p = p_ref[...]
    hi, lo = split2(p)
    p2 = jnp.concatenate([jnp.concatenate([hi, hi], 1), jnp.concatenate([lo, lo], 1)], 0)

    def put(start, width, value):
        z_ref[:, start : start + width] = value + refs[0][:, start : start + width] if len(refs) > 1 else value

    for k in range(2 * len(chunks)):
        start = pl.multiple_of(place_of(chunks[k // 2], k % 2, side) * piece, piece)
        m2 = jnp.concatenate(split2(merged_ref[:, pl.ds(start, piece)]), 0)
        part = dot(p2, m2, NN)
        put(k * piece, piece, part[:rank] + part[rank:])
    gram = lax.dot_general(p, p, NT, precision=HIGHEST, preferred_element_type=jnp.float32)
    put(2 * len(chunks) * piece, 128, jnp.concatenate([pack(gram), jnp.zeros((rank - rank * rank // 128, 128), jnp.float32)], 0))


def factor_kernel(gram_ref, p_ref, a_ref, *, replicas):
    rank = p_ref.shape[0]
    gram = unpack(gram_ref[...], rank)
    gram = jnp.concatenate([gram, jnp.zeros((rank, 128 - rank), jnp.float32)], 1)
    lane = lax.broadcasted_iota(jnp.int32, (rank, 128), 1)
    sub = lax.broadcasted_iota(jnp.int32, (rank, 128), 0)
    diagonal = jnp.where(lane == sub, gram, 0.0)
    by_row = 1.0 / jnp.sqrt(jnp.sum(diagonal, 1, keepdims=True))
    by_lane = jnp.where(lane[:1] < rank, 1.0 / jnp.sqrt(jnp.sum(diagonal, 0, keepdims=True)), 0.0)
    work = jnp.where(lane < rank, gram * by_row * by_lane, jnp.where(lane == sub + rank, by_row, 0.0))
    for j in range(0, rank - 2, 2):
        col0 = jnp.broadcast_to(work[:, j : j + 1], (rank, 128))
        col1 = jnp.broadcast_to(work[:, j + 1 : j + 2], (rank, 128))
        row0, row1 = work[j : j + 1, :], work[j + 1 : j + 2, :]
        a, b, c = col0[j : j + 1, :], col1[j : j + 1, :], col1[j + 1 : j + 2, :]
        scale = 1.0 / (a * c - b * b)
        step0, step1 = (c * row0 - b * row1) * scale, (a * row1 - b * row0) * scale
        below = sub > j + 1
        work = work - (jnp.where(below, col0, 0.0) * step0 + jnp.where(below, col1, 0.0) * step1)
    previous = jnp.concatenate([work[:1], work[:-1]], 0)
    low = jnp.sum(jnp.where(lane == sub - 1, work, 0.0), 1, keepdims=True)
    above = jnp.sum(jnp.where(lane == sub - 1, previous, 0.0), 1, keepdims=True)
    work = jnp.where(sub % 2 == 1, work - low / above * previous, work)
    pivots = jnp.sum(jnp.where(lane == sub, work, 0.0), 1, keepdims=True)
    inverse = (work / jnp.sqrt(pivots))[:, rank : 2 * rank]
    p_hat = lax.dot_general(inverse, p_ref[...], NN, precision=HIGHEST, preferred_element_type=jnp.float32)
    approx = lax.dot_general(p_hat, inverse, TN, precision=HIGHEST, preferred_element_type=jnp.float32) / replicas
    hi, lo = split2(jnp.concatenate([inverse, approx], 0))
    a_ref[...] = jnp.concatenate([hi, hi, lo], 1)


def finish_kernel(*refs, parts, earlier, piece, side):
    a_ref, own_ref, other_ref = refs[:3]
    z_refs = refs[3 : 3 + len(parts)]
    q_hbm, update_hbm, feedback_hbm, q_v, update_v, feedback_v, sems = refs[3 + len(parts) + earlier :]
    half = q_hbm.shape[1] // 2
    rank = q_v.shape[0]
    a = a_ref[...]
    copies = []
    k = 0
    for z_ref, (chunks, sibling) in zip(z_refs, parts):
        for h in range(2 * len(chunks)):
            hi, lo = split2(z_ref[:, h * piece : (h + 1) * piece])
            out = dot(a, jnp.concatenate([hi, lo, hi], 0), NN)
            here = pl.ds(k * piece, piece)
            place = place_of(chunks[h // 2], h % 2, side) * piece
            there = pl.ds(pl.multiple_of(((lax.axis_index("tensor") & 1) ^ sibling) * half + place, piece), piece)
            merged_ref = other_ref if sibling else own_ref
            approx = out[rank:]
            q_v[:, here] = out[:rank]
            update_v[:, here] = approx.astype(jnp.bfloat16)
            feedback_v[:, here] = (merged_ref[:, pl.ds(pl.multiple_of(place, piece), piece)] - approx).astype(jnp.bfloat16)
            for i, (local, whole) in enumerate([(q_v, q_hbm), (update_v, update_hbm), (feedback_v, feedback_hbm)]):
                copy = pltpu.make_async_copy(local.at[:, here], whole.at[:, there], sems.at[3 * k + i])
                copy.start()
                copies.append(copy)
            k += 1
    for copy in copies:
        copy.wait()


def grad_call(go, tokens, feedback, q, blocks=4):
    rows, toks = go.shape
    d = tokens.shape[1]
    rank = q.shape[0]
    return pl.pallas_call(
        functools.partial(grad_kernel, blocks=blocks),
        in_specs=[pl.BlockSpec(memory_space=pl.ANY)] * 4,
        out_specs=[pl.BlockSpec(memory_space=pltpu.VMEM)] * 3,
        out_shape=[
            jax.ShapeDtypeStruct((rows, d // 2), jnp.float32),
            jax.ShapeDtypeStruct((rows, d // 2), jnp.float32),
            jax.ShapeDtypeStruct((rank, rows), jnp.float32),
        ],
        scratch_shapes=[
            pltpu.VMEM((rows, toks), go.dtype),
            pltpu.VMEM((toks, d), tokens.dtype),
            pltpu.VMEM((rows, d), feedback.dtype),
            pltpu.VMEM((rank, d), q.dtype),
            pltpu.VMEM((d, 2 * rank), jnp.bfloat16),
            pltpu.SemaphoreType.DMA((3 + 2 * blocks,)),
        ],
        compiler_params=pltpu.CompilerParams(vmem_limit_bytes=24 * MIB),
        name="grad_and_p",
    )(*[in_hbm(x) for x in (go, tokens, feedback, q)])


def z_call(p, merged, chunks, piece, earlier, side, name):
    rank, rows = p.shape
    width = 2 * len(chunks) * piece
    return pl.pallas_call(
        functools.partial(z_kernel, chunks=chunks, piece=piece, side=side),
        in_specs=[pl.BlockSpec(memory_space=pltpu.VMEM)] * (2 + len(earlier)),
        out_specs=pl.BlockSpec(memory_space=pltpu.VMEM),
        out_shape=jax.ShapeDtypeStruct((rank, width + 128), jnp.float32),
        compiler_params=pltpu.CompilerParams(vmem_limit_bytes=16 * MIB),
        cost_estimate=pl.CostEstimate(flops=8 * rank * rows * width, bytes_accessed=2 * MIB, transcendentals=0),
        name=name,
    )(p, merged, *earlier)


def factor_call(gram, p, replicas):
    rank, rows = p.shape
    return pl.pallas_call(
        functools.partial(factor_kernel, replicas=replicas),
        in_specs=[pl.BlockSpec(memory_space=pltpu.VMEM)] * 2,
        out_specs=pl.BlockSpec(memory_space=pltpu.VMEM),
        out_shape=jax.ShapeDtypeStruct((rank + rows, 3 * rank), jnp.bfloat16),
        compiler_params=pltpu.CompilerParams(vmem_limit_bytes=8 * MIB),
        cost_estimate=pl.CostEstimate(flops=10**9, bytes_accessed=8 * MIB, transcendentals=0),
        name="factor",
    )(gram, p)


def finish_call(a, own, other, parts, d, piece, earlier, side, name):
    zs = [z for z, _, _ in parts]
    rank = zs[0].shape[0]
    rows = own.shape[0]
    width = sum(z.shape[1] for z in zs)
    vmem, anywhere = pl.BlockSpec(memory_space=pltpu.VMEM), pl.BlockSpec(memory_space=pl.ANY)
    return pl.pallas_call(
        functools.partial(
            finish_kernel,
            parts=[(chunks, sibling) for _, chunks, sibling in parts],
            earlier=len(earlier),
            piece=piece,
            side=side,
        ),
        in_specs=[vmem] * (3 + len(zs)) + [anywhere] * len(earlier),
        out_specs=[pl.BlockSpec(memory_space=pltpu.HBM)] * 3,
        out_shape=[
            jax.ShapeDtypeStruct((rank, d), jnp.float32),
            jax.ShapeDtypeStruct((rows, d), jnp.bfloat16),
            jax.ShapeDtypeStruct((rows, d), jnp.bfloat16),
        ],
        scratch_shapes=[
            pltpu.VMEM((rank, width), jnp.float32),
            pltpu.VMEM((rows, width), jnp.bfloat16),
            pltpu.VMEM((rows, width), jnp.bfloat16),
            pltpu.SemaphoreType.DMA((3 * width // piece,)),
        ],
        input_output_aliases={3 + len(zs) + i: i for i in range(len(earlier))},
        compiler_params=pltpu.CompilerParams(vmem_limit_bytes=16 * MIB),
        cost_estimate=pl.CostEstimate(flops=10**8, bytes_accessed=4 * MIB, transcendentals=0),
        name=name,
    )(a, own, other, *zs, *earlier)


def solution(mesh):
    replicas, shards = mesh.shape["dp"], mesh.shape["tensor"]
    devices = replicas * shards
    side = 1 << ((replicas.bit_length() - 1) // 2)
    core, near_x, near_y, near_z = 1, shards, side * shards, 2
    plane = [0, near_x, near_y, near_x | near_y]
    far_dp = [f * shards for f in (1 << b for b in range(replicas.bit_length() - 1)) if f not in (1, side)]
    far_tensor = [1 << b for b in range(2, shards.bit_length() - 1)]

    def flip(x, mask):
        return lax.ppermute(x, ("dp", "tensor"), [(i, i ^ mask) for i in range(devices)])

    def sum_dp(p):
        if replicas == 4:
            return (p + flip(p, near_x)) + (flip(p, near_y) + flip(p, near_x | near_y))
        for b in range(replicas.bit_length() - 1):
            p = p + flip(p, shards << b)
        return p

    def on_device(tokens, grad_out, feedback, q_prev):
        d = tokens.shape[1]
        chunk, piece = d // 8, d // 16
        own, other, p = grad_call(grad_out.T, tokens, feedback[0], q_prev.T)
        siblings = flip(other, core)
        p = sum_dp(p)
        chunks = (0, 3, 2, 1)
        z = z_call(p, own, chunks, piece, (), side, "z_own_rows")
        z = z_call(flip(p, core), siblings, chunks, piece, (z,), side, "z_sibling_rows")
        part = {c: z[:, k * chunk : (k + 1) * chunk] for k, c in enumerate(chunks)}
        rank = z.shape[0]
        gram = z[: rank * rank // 128, 4 * chunk :]
        total = (part[0] + flip(part[3], plane[3])) + (flip(part[2], plane[2]) + flip(part[1], plane[1]))
        size = rank * piece // 128
        given = jnp.concatenate([stack(total[:, piece:]), gram], 0)
        both = jnp.concatenate([stack(total[:, :piece]), gram], 0) + flip(given, near_z)
        total, gram = both[:size], both[size:]
        for mask in far_dp:
            total = total + flip(total, mask)
        both = jnp.concatenate([total, gram], 0)
        for mask in far_tensor:
            both = both + flip(both, mask)
        total, gram = both[:size], both[size:]
        a = factor_call(gram, p, replicas)
        whole = jnp.concatenate([unstack(total, rank), unstack(flip(total, near_z), rank)], 1)
        whole, a = lax.optimization_barrier((whole, a))
        got = {0: whole}
        for k in (3, 2, 1):
            got[k] = flip(whole, plane[k])
        outs = finish_call(a, own, other, [(got[0], (0,), 0), (got[3], (3,), 0)], d, piece, (), side, "finish_first")
        first = flip(jnp.concatenate([got[0], got[3]], 1), core)
        second, outs = lax.optimization_barrier((jnp.concatenate([got[2], got[1]], 1), outs))
        second = flip(second, core)
        outs = finish_call(a, own, other, [(got[2], (2,), 0), (got[1], (1,), 0)], d, piece, outs, side, "finish_second")
        q, update, new_feedback = finish_call(a, own, other, [(first, (0, 3), 1), (second, (2, 1), 1)], d, piece, outs, side, "finish_third")
        return q.T, update, new_feedback[None]

    return jax.shard_map(
        on_device,
        mesh=mesh,
        in_specs=(P("dp", None), P("dp", "tensor"), P("dp", "tensor", None), P()),
        out_specs=(P(), P("tensor", None), P("dp", "tensor", None)),
        check_vma=False,
    )
```

```python
import functools

import jax
import jax.numpy as jnp
from jax import lax
from jax.experimental import pallas as pl
from jax.experimental.pallas import tpu as pltpu
from jax.sharding import PartitionSpec as P

MIB = 1 << 20
HIGHEST = lax.Precision.HIGHEST
NN = (((1,), (0,)), ((), ()))
NT = (((1,), (1,)), ((), ()))
TN = (((0,), (0,)), ((), ()))


def split2(x):
    hi = x.astype(jnp.bfloat16)
    lo = (x - hi.astype(jnp.float32)).astype(jnp.bfloat16)
    return hi, lo


def dot(a, b, dims):
    return lax.dot_general(a, b, dims, preferred_element_type=jnp.float32)


def pack(x):
    parts, rows = 128 // x.shape[1], x.shape[0] * x.shape[1] // 128
    return jnp.concatenate([x[i * rows : (i + 1) * rows] for i in range(parts)], 1)


def unpack(x, rank):
    return jnp.concatenate([x[:, i * rank : (i + 1) * rank] for i in range(128 // rank)], 0)


def stack(x):
    return jnp.concatenate([x[:, i : i + 128] for i in range(0, x.shape[1], 128)], 0)


def unstack(x, rank):
    return jnp.concatenate([x[i : i + rank] for i in range(0, x.shape[0], rank)], 1)


def in_hbm(x):
    return pltpu.with_memory_space_constraint(x, pltpu.HBM)


def grad_kernel(go_hbm, tok_hbm, fb_hbm, q_hbm, own_ref, other_ref, p_ref, go_v, tok_v, fb_v, q_v, qt_v, sems, *, blocks):
    rank, rows = p_ref.shape
    d = tok_hbm.shape[1]
    width = d // blocks
    core = lax.axis_index("tensor") & 1
    copy_go = pltpu.make_async_copy(go_hbm, go_v, sems.at[0])
    copy_go.start()
    copies_q = []
    for k in range(2):
        there = pl.ds(pl.multiple_of((core ^ k) * (d // 2), d // 2), d // 2)
        copies_q.append(pltpu.make_async_copy(q_hbm.at[:, there], q_v.at[:, pl.ds(k * (d // 2), d // 2)], sems.at[1 + k]))
        copies_q[k].start()
    copies = []
    for k in range(blocks):
        start = (core ^ (2 * k // blocks)) * (d // 2) + k % (blocks // 2) * width
        there = pl.ds(pl.multiple_of(start, width), width)
        block = [
            pltpu.make_async_copy(whole.at[:, there], local.at[:, pl.ds(k * width, width)], sems.at[3 + 2 * k + i])
            for i, (whole, local) in enumerate([(fb_hbm, fb_v), (tok_hbm, tok_v)])
        ]
        for copy in block:
            copy.start()
        copies.append(block)
    copy_go.wait()
    go = go_v[...]
    for copy in copies_q:
        copy.wait()
    for k in range(blocks):
        q2 = jnp.concatenate(split2(q_v[:, k * width : (k + 1) * width]), 0)
        qt_v[k * width : (k + 1) * width, :] = q2.T
    total = None
    for k in range(blocks):
        for copy in copies[k]:
            copy.wait()
        part = pl.ds(k * width, width)
        merged = dot(go, tok_v[:, part], NN) + fb_v[:, part].astype(jnp.float32)
        half_ref = own_ref if 2 * k < blocks else other_ref
        half_ref[:, pl.ds(k % (blocks // 2) * width, width)] = merged
        term = dot(jnp.concatenate(split2(merged), 0), qt_v[part, :], NN)
        total = term if total is None else total + term
    total = total[:, :rank] + total[:, rank:]
    p_ref[...] = (total[:rows] + total[rows:]).T


def place_of(chunk, h, side):
    dp, tensor = lax.axis_index("dp"), lax.axis_index("tensor")
    x, y, z = dp & 1, (dp // side) & 1, (tensor >> 1) & 1
    return (y ^ (chunk >> 1)) * 4 + (x ^ (chunk & 1)) * 2 + (z ^ h)


def z_kernel(p_ref, merged_ref, *refs, chunks, piece, side):
    z_ref = refs[-1]
    rank, rows = p_ref.shape
    p = p_ref[...]
    hi, lo = split2(p)
    p2 = jnp.concatenate([jnp.concatenate([hi, hi], 1), jnp.concatenate([lo, lo], 1)], 0)

    def put(start, width, value):
        z_ref[:, start : start + width] = value + refs[0][:, start : start + width] if len(refs) > 1 else value

    for k in range(2 * len(chunks)):
        start = pl.multiple_of(place_of(chunks[k // 2], k % 2, side) * piece, piece)
        m2 = jnp.concatenate(split2(merged_ref[:, pl.ds(start, piece)]), 0)
        part = dot(p2, m2, NN)
        put(k * piece, piece, part[:rank] + part[rank:])


def gram_kernel(p_ref, sibling_ref, gram_ref):
    gram_ref[...] = pack(
        sum(
            lax.dot_general(x[...], x[...], NT, precision=HIGHEST, preferred_element_type=jnp.float32)
            for x in (p_ref, sibling_ref)
        )
    )


def factor_kernel(gram_ref, p_ref, a_ref, *, replicas):
    rank = p_ref.shape[0]
    gram = unpack(gram_ref[...], rank)
    gram = jnp.concatenate([gram, jnp.zeros((rank, 128 - rank), jnp.float32)], 1)
    lane = lax.broadcasted_iota(jnp.int32, (rank, 128), 1)
    sub = lax.broadcasted_iota(jnp.int32, (rank, 128), 0)
    diagonal = jnp.where(lane == sub, gram, 0.0)
    by_row = 1.0 / jnp.sqrt(jnp.sum(diagonal, 1, keepdims=True))
    by_lane = jnp.where(lane[:1] < rank, 1.0 / jnp.sqrt(jnp.sum(diagonal, 0, keepdims=True)), 0.0)
    work = jnp.where(lane < rank, gram * by_row * by_lane, jnp.where(lane == sub + rank, by_row, 0.0))
    for j in range(0, rank - 2, 2):
        col0 = jnp.broadcast_to(work[:, j : j + 1], (rank, 128))
        col1 = jnp.broadcast_to(work[:, j + 1 : j + 2], (rank, 128))
        row0, row1 = work[j : j + 1, :], work[j + 1 : j + 2, :]
        a, b, c = col0[j : j + 1, :], col1[j : j + 1, :], col1[j + 1 : j + 2, :]
        scale = 1.0 / (a * c - b * b)
        step0, step1 = (c * row0 - b * row1) * scale, (a * row1 - b * row0) * scale
        below = sub > j + 1
        work = work - (jnp.where(below, col0, 0.0) * step0 + jnp.where(below, col1, 0.0) * step1)
    previous = jnp.concatenate([work[:1], work[:-1]], 0)
    low = jnp.sum(jnp.where(lane == sub - 1, work, 0.0), 1, keepdims=True)
    above = jnp.sum(jnp.where(lane == sub - 1, previous, 0.0), 1, keepdims=True)
    work = jnp.where(sub % 2 == 1, work - low / above * previous, work)
    pivots = jnp.sum(jnp.where(lane == sub, work, 0.0), 1, keepdims=True)
    inverse = (work / jnp.sqrt(pivots))[:, rank : 2 * rank]
    p_hat = lax.dot_general(inverse, p_ref[...], NN, precision=HIGHEST, preferred_element_type=jnp.float32)
    approx = lax.dot_general(p_hat, inverse, TN, precision=HIGHEST, preferred_element_type=jnp.float32) / replicas
    hi, lo = split2(jnp.concatenate([inverse, approx], 0))
    a_ref[...] = jnp.concatenate([hi, hi, lo], 1)


def finish_kernel(*refs, parts, earlier, piece, side):
    a_ref, own_ref, other_ref = refs[:3]
    z_refs = refs[3 : 3 + len(parts)]
    q_hbm, update_hbm, feedback_hbm, q_v, update_v, feedback_v, sems = refs[3 + len(parts) + earlier :]
    half = q_hbm.shape[1] // 2
    rank = q_v.shape[0]
    a = a_ref[...]
    copies = []
    k = 0
    for z_ref, (chunks, sibling) in zip(z_refs, parts):
        for h in range(2 * len(chunks)):
            hi, lo = split2(z_ref[:, h * piece : (h + 1) * piece])
            out = dot(a, jnp.concatenate([hi, lo, hi], 0), NN)
            here = pl.ds(k * piece, piece)
            place = place_of(chunks[h // 2], h % 2, side) * piece
            there = pl.ds(pl.multiple_of(((lax.axis_index("tensor") & 1) ^ sibling) * half + place, piece), piece)
            merged_ref = other_ref if sibling else own_ref
            approx = out[rank:]
            q_v[:, here] = out[:rank]
            update_v[:, here] = approx.astype(jnp.bfloat16)
            feedback_v[:, here] = (merged_ref[:, pl.ds(pl.multiple_of(place, piece), piece)] - approx).astype(jnp.bfloat16)
            for i, (local, whole) in enumerate([(q_v, q_hbm), (update_v, update_hbm), (feedback_v, feedback_hbm)]):
                copy = pltpu.make_async_copy(local.at[:, here], whole.at[:, there], sems.at[3 * k + i])
                copy.start()
                copies.append(copy)
            k += 1
    for copy in copies:
        copy.wait()


def grad_call(go, tokens, feedback, q, blocks=4):
    rows, toks = go.shape
    d = tokens.shape[1]
    rank = q.shape[0]
    return pl.pallas_call(
        functools.partial(grad_kernel, blocks=blocks),
        in_specs=[pl.BlockSpec(memory_space=pl.ANY)] * 4,
        out_specs=[pl.BlockSpec(memory_space=pltpu.VMEM)] * 3,
        out_shape=[
            jax.ShapeDtypeStruct((rows, d // 2), jnp.float32),
            jax.ShapeDtypeStruct((rows, d // 2), jnp.float32),
            jax.ShapeDtypeStruct((rank, rows), jnp.float32),
        ],
        scratch_shapes=[
            pltpu.VMEM((rows, toks), go.dtype),
            pltpu.VMEM((toks, d), tokens.dtype),
            pltpu.VMEM((rows, d), feedback.dtype),
            pltpu.VMEM((rank, d), q.dtype),
            pltpu.VMEM((d, 2 * rank), jnp.bfloat16),
            pltpu.SemaphoreType.DMA((3 + 2 * blocks,)),
        ],
        compiler_params=pltpu.CompilerParams(vmem_limit_bytes=24 * MIB),
        name="grad_and_p",
    )(*[in_hbm(x) for x in (go, tokens, feedback, q)])


def z_call(p, merged, chunks, piece, earlier, side, name):
    rank, rows = p.shape
    width = 2 * len(chunks) * piece
    return pl.pallas_call(
        functools.partial(z_kernel, chunks=chunks, piece=piece, side=side),
        in_specs=[pl.BlockSpec(memory_space=pltpu.VMEM)] * (2 + len(earlier)),
        out_specs=pl.BlockSpec(memory_space=pltpu.VMEM),
        out_shape=jax.ShapeDtypeStruct((rank, width), jnp.float32),
        compiler_params=pltpu.CompilerParams(vmem_limit_bytes=16 * MIB),
        cost_estimate=pl.CostEstimate(flops=8 * rank * rows * width, bytes_accessed=2 * MIB, transcendentals=0),
        name=name,
    )(p, merged, *earlier)


def gram_call(p, p_sibling):
    rank = p.shape[0]
    return pl.pallas_call(
        gram_kernel,
        in_specs=[pl.BlockSpec(memory_space=pltpu.VMEM)] * 2,
        out_specs=pl.BlockSpec(memory_space=pltpu.VMEM),
        out_shape=jax.ShapeDtypeStruct((rank * rank // 128, 128), jnp.float32),
        compiler_params=pltpu.CompilerParams(vmem_limit_bytes=8 * MIB),
        cost_estimate=pl.CostEstimate(flops=10**8, bytes_accessed=MIB, transcendentals=0),
        name="gram",
    )(p, p_sibling)


def factor_call(gram, p, replicas):
    rank, rows = p.shape
    return pl.pallas_call(
        functools.partial(factor_kernel, replicas=replicas),
        in_specs=[pl.BlockSpec(memory_space=pltpu.VMEM)] * 2,
        out_specs=pl.BlockSpec(memory_space=pltpu.VMEM),
        out_shape=jax.ShapeDtypeStruct((rank + rows, 3 * rank), jnp.bfloat16),
        compiler_params=pltpu.CompilerParams(vmem_limit_bytes=8 * MIB),
        cost_estimate=pl.CostEstimate(flops=10**9, bytes_accessed=8 * MIB, transcendentals=0),
        name="factor",
    )(gram, p)


def finish_call(a, own, other, parts, d, piece, earlier, side, name):
    zs = [z for z, _, _ in parts]
    rank = zs[0].shape[0]
    rows = own.shape[0]
    width = sum(z.shape[1] for z in zs)
    vmem, anywhere = pl.BlockSpec(memory_space=pltpu.VMEM), pl.BlockSpec(memory_space=pl.ANY)
    return pl.pallas_call(
        functools.partial(
            finish_kernel,
            parts=[(chunks, sibling) for _, chunks, sibling in parts],
            earlier=len(earlier),
            piece=piece,
            side=side,
        ),
        in_specs=[vmem] * (3 + len(zs)) + [anywhere] * len(earlier),
        out_specs=[pl.BlockSpec(memory_space=pltpu.HBM)] * 3,
        out_shape=[
            jax.ShapeDtypeStruct((rank, d), jnp.float32),
            jax.ShapeDtypeStruct((rows, d), jnp.bfloat16),
            jax.ShapeDtypeStruct((rows, d), jnp.bfloat16),
        ],
        scratch_shapes=[
            pltpu.VMEM((rank, width), jnp.float32),
            pltpu.VMEM((rows, width), jnp.bfloat16),
            pltpu.VMEM((rows, width), jnp.bfloat16),
            pltpu.SemaphoreType.DMA((3 * width // piece,)),
        ],
        input_output_aliases={3 + len(zs) + i: i for i in range(len(earlier))},
        compiler_params=pltpu.CompilerParams(vmem_limit_bytes=16 * MIB),
        cost_estimate=pl.CostEstimate(flops=10**8, bytes_accessed=4 * MIB, transcendentals=0),
        name=name,
    )(a, own, other, *zs, *earlier)


def solution(mesh):
    replicas, shards = mesh.shape["dp"], mesh.shape["tensor"]
    devices = replicas * shards
    side = 1 << ((replicas.bit_length() - 1) // 2)
    core, near_x, near_y, near_z = 1, shards, side * shards, 2
    plane = [0, near_x, near_y, near_x | near_y]
    far_dp = [f * shards for f in (1 << b for b in range(replicas.bit_length() - 1)) if f not in (1, side)]
    far_tensor = [1 << b for b in range(2, shards.bit_length() - 1)]

    def flip(x, mask):
        return lax.ppermute(x, ("dp", "tensor"), [(i, i ^ mask) for i in range(devices)])

    def sum_dp(p):
        if replicas == 4:
            return (p + flip(p, near_x)) + (flip(p, near_y) + flip(p, near_x | near_y))
        for b in range(replicas.bit_length() - 1):
            p = p + flip(p, shards << b)
        return p

    def on_device(tokens, grad_out, feedback, q_prev):
        d = tokens.shape[1]
        chunk, piece = d // 8, d // 16
        own, other, p = grad_call(grad_out.T, tokens, feedback[0], q_prev.T)
        siblings = flip(other, core)
        p = sum_dp(p)
        chunks = (0, 3, 2, 1)
        p_sibling = flip(p, core)
        z = z_call(p, own, chunks, piece, (), side, "z_own_rows")
        z = z_call(p_sibling, siblings, chunks, piece, (z,), side, "z_sibling_rows")
        part = {c: z[:, k * chunk : (k + 1) * chunk] for k, c in enumerate(chunks)}
        rank = z.shape[0]
        gram = gram_call(p, p_sibling)
        total = (part[0] + flip(part[3], plane[3])) + (flip(part[2], plane[2]) + flip(part[1], plane[1]))
        size = rank * piece // 128
        given = jnp.concatenate([stack(total[:, piece:]), gram], 0)
        both = jnp.concatenate([stack(total[:, :piece]), gram], 0) + flip(given, near_z)
        total, gram = both[:size], both[size:]
        for mask in far_dp:
            total = total + flip(total, mask)
        both = jnp.concatenate([total, gram], 0)
        for mask in far_tensor:
            both = both + flip(both, mask)
        total, gram = both[:size], both[size:]
        a = factor_call(gram, p, replicas)
        whole = jnp.concatenate([unstack(total, rank), unstack(flip(total, near_z), rank)], 1)
        whole, a = lax.optimization_barrier((whole, a))
        got = {0: whole}
        for k in (3, 2, 1):
            got[k] = flip(whole, plane[k])
        outs = finish_call(a, own, other, [(got[0], (0,), 0), (got[3], (3,), 0)], d, piece, (), side, "finish_first")
        first = flip(jnp.concatenate([got[0], got[3]], 1), core)
        second, outs = lax.optimization_barrier((jnp.concatenate([got[2], got[1]], 1), outs))
        second = flip(second, core)
        outs = finish_call(a, own, other, [(got[2], (2,), 0), (got[1], (1,), 0)], d, piece, outs, side, "finish_second")
        q, update, new_feedback = finish_call(a, own, other, [(first, (0, 3), 1), (second, (2, 1), 1)], d, piece, outs, side, "finish_third")
        return q.T, update, new_feedback[None]

    return jax.shard_map(
        on_device,
        mesh=mesh,
        in_specs=(P("dp", None), P("dp", "tensor"), P("dp", "tensor", None), P()),
        out_specs=(P(), P("tensor", None), P("dp", "tensor", None)),
        check_vma=False,
    )
```

```python
import functools

import jax
import jax.numpy as jnp
from jax import lax
from jax.experimental import pallas as pl
from jax.experimental.pallas import tpu as pltpu
from jax.sharding import PartitionSpec as P

MIB = 1 << 20
HIGHEST = lax.Precision.HIGHEST
NN = (((1,), (0,)), ((), ()))
NT = (((1,), (1,)), ((), ()))
TN = (((0,), (0,)), ((), ()))


def split2(x):
    hi = x.astype(jnp.bfloat16)
    lo = (x - hi.astype(jnp.float32)).astype(jnp.bfloat16)
    return hi, lo


def dot(a, b, dims):
    return lax.dot_general(a, b, dims, preferred_element_type=jnp.float32)


def pack(x):
    parts, rows = 128 // x.shape[1], x.shape[0] * x.shape[1] // 128
    return jnp.concatenate([x[i * rows : (i + 1) * rows] for i in range(parts)], 1)


def unpack(x, rank):
    return jnp.concatenate([x[:, i * rank : (i + 1) * rank] for i in range(128 // rank)], 0)


def stack(x):
    return jnp.concatenate([x[:, i : i + 128] for i in range(0, x.shape[1], 128)], 0)


def unstack(x, rank):
    return jnp.concatenate([x[i : i + rank] for i in range(0, x.shape[0], rank)], 1)


def in_hbm(x):
    return pltpu.with_memory_space_constraint(x, pltpu.HBM)


def grad_kernel(go_hbm, tok_hbm, fb_hbm, q_hbm, own_ref, other_ref, p_ref, go_v, tok_v, fb_v, q_v, qt_v, sems, *, blocks):
    rank, rows = p_ref.shape
    d = tok_hbm.shape[1]
    width = d // blocks
    core = lax.axis_index("tensor") & 1
    copy_go = pltpu.make_async_copy(go_hbm, go_v, sems.at[0])
    copy_go.start()
    copies_q = []
    for k in range(2):
        there = pl.ds(pl.multiple_of((core ^ k) * (d // 2), d // 2), d // 2)
        copies_q.append(pltpu.make_async_copy(q_hbm.at[:, there], q_v.at[:, pl.ds(k * (d // 2), d // 2)], sems.at[1 + k]))
        copies_q[k].start()
    copies = []
    for k in range(blocks):
        start = (core ^ (2 * k // blocks)) * (d // 2) + k % (blocks // 2) * width
        there = pl.ds(pl.multiple_of(start, width), width)
        block = [
            pltpu.make_async_copy(whole.at[:, there], local.at[:, pl.ds(k * width, width)], sems.at[3 + 2 * k + i])
            for i, (whole, local) in enumerate([(fb_hbm, fb_v), (tok_hbm, tok_v)])
        ]
        for copy in block:
            copy.start()
        copies.append(block)
    copy_go.wait()
    go = go_v[...]
    for copy in copies_q:
        copy.wait()
    for k in range(blocks):
        q2 = jnp.concatenate(split2(q_v[:, k * width : (k + 1) * width]), 0)
        qt_v[k * width : (k + 1) * width, :] = q2.T
    total = None
    for k in range(blocks):
        for copy in copies[k]:
            copy.wait()
        part = pl.ds(k * width, width)
        merged = dot(go, tok_v[:, part], NN) + fb_v[:, part].astype(jnp.float32)
        half_ref = own_ref if 2 * k < blocks else other_ref
        half_ref[:, pl.ds(k % (blocks // 2) * width, width)] = merged
        term = dot(jnp.concatenate(split2(merged), 0), qt_v[part, :], NN)
        total = term if total is None else total + term
    total = total[:, :rank] + total[:, rank:]
    p_ref[...] = (total[:rows] + total[rows:]).T


def place_of(chunk, h, side):
    dp, tensor = lax.axis_index("dp"), lax.axis_index("tensor")
    x, y, z = dp & 1, (dp // side) & 1, (tensor >> 1) & 1
    return (y ^ (chunk >> 1)) * 4 + (x ^ (chunk & 1)) * 2 + (z ^ h)


def z_kernel(p_ref, merged_ref, *refs, chunks, piece, side):
    z_ref = refs[-1]
    rank, rows = p_ref.shape
    p = p_ref[...]
    hi, lo = split2(p)
    p2 = jnp.concatenate([jnp.concatenate([hi, hi], 1), jnp.concatenate([lo, lo], 1)], 0)

    def put(start, width, value):
        z_ref[:, start : start + width] = value + refs[0][:, start : start + width] if len(refs) > 1 else value

    for k in range(2 * len(chunks)):
        start = pl.multiple_of(place_of(chunks[k // 2], k % 2, side) * piece, piece)
        m2 = jnp.concatenate(split2(merged_ref[:, pl.ds(start, piece)]), 0)
        part = dot(p2, m2, NN)
        put(k * piece, piece, part[:rank] + part[rank:])


def gram_kernel(p_ref, sibling_ref, gram_ref):
    gram_ref[...] = pack(
        sum(
            lax.dot_general(x[...], x[...], NT, precision=HIGHEST, preferred_element_type=jnp.float32)
            for x in (p_ref, sibling_ref)
        )
    )


def factor_kernel(gram_ref, p_ref, a_ref, *, replicas):
    rank = p_ref.shape[0]
    gram = unpack(gram_ref[...], rank)
    gram = jnp.concatenate([gram, jnp.zeros((rank, 128 - rank), jnp.float32)], 1)
    lane = lax.broadcasted_iota(jnp.int32, (rank, 128), 1)
    sub = lax.broadcasted_iota(jnp.int32, (rank, 128), 0)
    diagonal = jnp.where(lane == sub, gram, 0.0)
    by_row = 1.0 / jnp.sqrt(jnp.sum(diagonal, 1, keepdims=True))
    by_lane = jnp.where(lane[:1] < rank, 1.0 / jnp.sqrt(jnp.sum(diagonal, 0, keepdims=True)), 0.0)
    work = jnp.where(lane < rank, gram * by_row * by_lane, jnp.where(lane == sub + rank, by_row, 0.0))
    for j in range(0, rank - 2, 2):
        col0 = jnp.broadcast_to(work[:, j : j + 1], (rank, 128))
        col1 = jnp.broadcast_to(work[:, j + 1 : j + 2], (rank, 128))
        row0, row1 = work[j : j + 1, :], work[j + 1 : j + 2, :]
        a, b, c = col0[j : j + 1, :], col1[j : j + 1, :], col1[j + 1 : j + 2, :]
        scale = 1.0 / (a * c - b * b)
        step0, step1 = (c * row0 - b * row1) * scale, (a * row1 - b * row0) * scale
        below = sub > j + 1
        work = work - (jnp.where(below, col0, 0.0) * step0 + jnp.where(below, col1, 0.0) * step1)
    previous = jnp.concatenate([work[:1], work[:-1]], 0)
    low = jnp.sum(jnp.where(lane == sub - 1, work, 0.0), 1, keepdims=True)
    above = jnp.sum(jnp.where(lane == sub - 1, previous, 0.0), 1, keepdims=True)
    work = jnp.where(sub % 2 == 1, work - low / above * previous, work)
    pivots = jnp.sum(jnp.where(lane == sub, work, 0.0), 1, keepdims=True)
    inverse = (work / jnp.sqrt(pivots))[:, rank : 2 * rank]
    p_hat = lax.dot_general(inverse, p_ref[...], NN, precision=HIGHEST, preferred_element_type=jnp.float32)
    approx = lax.dot_general(p_hat, inverse, TN, precision=HIGHEST, preferred_element_type=jnp.float32) / replicas
    hi, lo = split2(jnp.concatenate([inverse, approx], 0))
    a_ref[...] = jnp.concatenate([hi, hi, lo], 1)


def finish_kernel(*refs, parts, earlier, piece, side):
    a_ref, own_ref, other_ref = refs[:3]
    z_refs = refs[3 : 3 + len(parts)]
    q_hbm, update_hbm, feedback_hbm, q_v, update_v, feedback_v, sems = refs[3 + len(parts) + earlier :]
    half = q_hbm.shape[1] // 2
    rank = q_v.shape[0]
    a = a_ref[...]
    copies = []
    k = 0
    for z_ref, (chunks, sibling) in zip(z_refs, parts):
        for h in range(2 * len(chunks)):
            hi, lo = split2(z_ref[:, h * piece : (h + 1) * piece])
            out = dot(a, jnp.concatenate([hi, lo, hi], 0), NN)
            here = pl.ds(k * piece, piece)
            place = place_of(chunks[h // 2], h % 2, side) * piece
            there = pl.ds(pl.multiple_of(((lax.axis_index("tensor") & 1) ^ sibling) * half + place, piece), piece)
            merged_ref = other_ref if sibling else own_ref
            approx = out[rank:]
            q_v[:, here] = out[:rank]
            update_v[:, here] = approx.astype(jnp.bfloat16)
            feedback_v[:, here] = (merged_ref[:, pl.ds(pl.multiple_of(place, piece), piece)] - approx).astype(jnp.bfloat16)
            for i, (local, whole) in enumerate([(q_v, q_hbm), (update_v, update_hbm), (feedback_v, feedback_hbm)]):
                copy = pltpu.make_async_copy(local.at[:, here], whole.at[:, there], sems.at[3 * k + i])
                copy.start()
                copies.append(copy)
            k += 1
    for copy in copies:
        copy.wait()


def grad_call(go, tokens, feedback, q, blocks=4):
    rows, toks = go.shape
    d = tokens.shape[1]
    rank = q.shape[0]
    return pl.pallas_call(
        functools.partial(grad_kernel, blocks=blocks),
        in_specs=[pl.BlockSpec(memory_space=pl.ANY)] * 4,
        out_specs=[pl.BlockSpec(memory_space=pltpu.VMEM)] * 3,
        out_shape=[
            jax.ShapeDtypeStruct((rows, d // 2), jnp.float32),
            jax.ShapeDtypeStruct((rows, d // 2), jnp.float32),
            jax.ShapeDtypeStruct((rank, rows), jnp.float32),
        ],
        scratch_shapes=[
            pltpu.VMEM((rows, toks), go.dtype),
            pltpu.VMEM((toks, d), tokens.dtype),
            pltpu.VMEM((rows, d), feedback.dtype),
            pltpu.VMEM((rank, d), q.dtype),
            pltpu.VMEM((d, 2 * rank), jnp.bfloat16),
            pltpu.SemaphoreType.DMA((3 + 2 * blocks,)),
        ],
        compiler_params=pltpu.CompilerParams(vmem_limit_bytes=24 * MIB),
        name="grad_and_p",
    )(*[in_hbm(x) for x in (go, tokens, feedback, q)])


def z_call(p, merged, chunks, piece, earlier, side, name):
    rank, rows = p.shape
    width = 2 * len(chunks) * piece
    return pl.pallas_call(
        functools.partial(z_kernel, chunks=chunks, piece=piece, side=side),
        in_specs=[pl.BlockSpec(memory_space=pltpu.VMEM)] * (2 + len(earlier)),
        out_specs=pl.BlockSpec(memory_space=pltpu.VMEM),
        out_shape=jax.ShapeDtypeStruct((rank, width), jnp.float32),
        compiler_params=pltpu.CompilerParams(vmem_limit_bytes=16 * MIB),
        cost_estimate=pl.CostEstimate(flops=8 * rank * rows * width, bytes_accessed=2 * MIB, transcendentals=0),
        name=name,
    )(p, merged, *earlier)


def gram_call(p, p_sibling):
    rank = p.shape[0]
    return pl.pallas_call(
        gram_kernel,
        in_specs=[pl.BlockSpec(memory_space=pltpu.VMEM)] * 2,
        out_specs=pl.BlockSpec(memory_space=pltpu.VMEM),
        out_shape=jax.ShapeDtypeStruct((rank * rank // 128, 128), jnp.float32),
        compiler_params=pltpu.CompilerParams(vmem_limit_bytes=8 * MIB),
        cost_estimate=pl.CostEstimate(flops=10**8, bytes_accessed=MIB, transcendentals=0),
        name="gram",
    )(p, p_sibling)


def factor_call(gram, p, replicas):
    rank, rows = p.shape
    return pl.pallas_call(
        functools.partial(factor_kernel, replicas=replicas),
        in_specs=[pl.BlockSpec(memory_space=pltpu.VMEM)] * 2,
        out_specs=pl.BlockSpec(memory_space=pltpu.VMEM),
        out_shape=jax.ShapeDtypeStruct((rank + rows, 3 * rank), jnp.bfloat16),
        compiler_params=pltpu.CompilerParams(vmem_limit_bytes=8 * MIB),
        cost_estimate=pl.CostEstimate(flops=10**9, bytes_accessed=8 * MIB, transcendentals=0),
        name="factor",
    )(gram, p)


def finish_call(a, own, other, parts, d, piece, earlier, side, name):
    zs = [z for z, _, _ in parts]
    rank = zs[0].shape[0]
    rows = own.shape[0]
    width = sum(z.shape[1] for z in zs)
    vmem, anywhere = pl.BlockSpec(memory_space=pltpu.VMEM), pl.BlockSpec(memory_space=pl.ANY)
    return pl.pallas_call(
        functools.partial(
            finish_kernel,
            parts=[(chunks, sibling) for _, chunks, sibling in parts],
            earlier=len(earlier),
            piece=piece,
            side=side,
        ),
        in_specs=[vmem] * (3 + len(zs)) + [anywhere] * len(earlier),
        out_specs=[pl.BlockSpec(memory_space=pltpu.HBM)] * 3,
        out_shape=[
            jax.ShapeDtypeStruct((rank, d), jnp.float32),
            jax.ShapeDtypeStruct((rows, d), jnp.bfloat16),
            jax.ShapeDtypeStruct((rows, d), jnp.bfloat16),
        ],
        scratch_shapes=[
            pltpu.VMEM((rank, width), jnp.float32),
            pltpu.VMEM((rows, width), jnp.bfloat16),
            pltpu.VMEM((rows, width), jnp.bfloat16),
            pltpu.SemaphoreType.DMA((3 * width // piece,)),
        ],
        input_output_aliases={3 + len(zs) + i: i for i in range(len(earlier))},
        compiler_params=pltpu.CompilerParams(vmem_limit_bytes=16 * MIB),
        cost_estimate=pl.CostEstimate(flops=10**8, bytes_accessed=4 * MIB, transcendentals=0),
        name=name,
    )(a, own, other, *zs, *earlier)


def solution(mesh):
    replicas, shards = mesh.shape["dp"], mesh.shape["tensor"]
    devices = replicas * shards
    side = 1 << ((replicas.bit_length() - 1) // 2)
    core, near_x, near_y, near_z = 1, shards, side * shards, 2
    plane = [0, near_x, near_y, near_x | near_y]
    far_dp = [f * shards for f in (1 << b for b in range(replicas.bit_length() - 1)) if f not in (1, side)]
    far_tensor = [1 << b for b in range(2, shards.bit_length() - 1)]

    def flip(x, mask):
        return lax.ppermute(x, ("dp", "tensor"), [(i, i ^ mask) for i in range(devices)])

    def sum_dp(p):
        if replicas == 4:
            return (p + flip(p, near_x)) + (flip(p, near_y) + flip(p, near_x | near_y))
        for b in range(replicas.bit_length() - 1):
            p = p + flip(p, shards << b)
        return p

    def on_device(tokens, grad_out, feedback, q_prev):
        d = tokens.shape[1]
        chunk, piece = d // 8, d // 16
        own, other, p = grad_call(grad_out.T, tokens, feedback[0], q_prev.T)
        siblings = flip(other, core)
        p = sum_dp(p)
        p_sibling = flip(p, core)
        z = z_call(p, own, (3,), piece, (), side, "z_own_far")
        rest = z_call(p, own, (0, 2, 1), piece, (), side, "z_own_near")
        z, p_late = lax.optimization_barrier((z_call(p_sibling, siblings, (3,), piece, (z,), side, "z_sibling_far"), p_sibling))
        rest = z_call(p_late, siblings, (0, 2, 1), piece, (rest,), side, "z_sibling_near")
        part = {3: z, **{c: rest[:, k * chunk : (k + 1) * chunk] for k, c in enumerate((0, 2, 1))}}
        rank = z.shape[0]
        gram = gram_call(p, p_sibling)
        near = flip(part[1], plane[1])
        total = (part[0] + near) + (flip(part[2], plane[2]) + flip(part[3], plane[3]))
        size = rank * piece // 128
        given = jnp.concatenate([stack(total[:, piece:]), gram], 0)
        both = jnp.concatenate([stack(total[:, :piece]), gram], 0) + flip(given, near_z)
        total, gram = both[:size], both[size:]
        for mask in far_dp:
            total = total + flip(total, mask)
        both = jnp.concatenate([total, gram], 0)
        for mask in far_tensor:
            both = both + flip(both, mask)
        total, gram = both[:size], both[size:]
        a = factor_call(gram, p, replicas)
        whole = jnp.concatenate([unstack(total, rank), unstack(flip(total, near_z), rank)], 1)
        whole, a = lax.optimization_barrier((whole, a))
        got = {0: whole}
        for k in (3, 2, 1):
            got[k] = flip(whole, plane[k])
        outs = finish_call(a, own, other, [(got[0], (0,), 0), (got[3], (3,), 0)], d, piece, (), side, "finish_first")
        first = flip(jnp.concatenate([got[0], got[3]], 1), core)
        second, outs = lax.optimization_barrier((jnp.concatenate([got[2], got[1]], 1), outs))
        second = flip(second, core)
        outs = finish_call(a, own, other, [(got[2], (2,), 0), (got[1], (1,), 0)], d, piece, outs, side, "finish_second")
        q, update, new_feedback = finish_call(a, own, other, [(first, (0, 3), 1), (second, (2, 1), 1)], d, piece, outs, side, "finish_third")
        return q.T, update, new_feedback[None]

    return jax.shard_map(
        on_device,
        mesh=mesh,
        in_specs=(P("dp", None), P("dp", "tensor"), P("dp", "tensor", None), P()),
        out_specs=(P(), P("tensor", None), P("dp", "tensor", None)),
        check_vma=False,
    )
```

```python
import functools

import jax
import jax.numpy as jnp
from jax import lax
from jax.experimental import pallas as pl
from jax.experimental.pallas import tpu as pltpu
from jax.sharding import PartitionSpec as P

MIB = 1 << 20
HIGHEST = lax.Precision.HIGHEST
NN = (((1,), (0,)), ((), ()))
NT = (((1,), (1,)), ((), ()))
TN = (((0,), (0,)), ((), ()))


def split2(x):
    hi = x.astype(jnp.bfloat16)
    lo = (x - hi.astype(jnp.float32)).astype(jnp.bfloat16)
    return hi, lo


def dot(a, b, dims):
    return lax.dot_general(a, b, dims, preferred_element_type=jnp.float32)


def pack(x):
    parts, rows = 128 // x.shape[1], x.shape[0] * x.shape[1] // 128
    return jnp.concatenate([x[i * rows : (i + 1) * rows] for i in range(parts)], 1)


def unpack(x, rank):
    return jnp.concatenate([x[:, i * rank : (i + 1) * rank] for i in range(128 // rank)], 0)


def stack(x):
    return jnp.concatenate([x[:, i : i + 128] for i in range(0, x.shape[1], 128)], 0)


def unstack(x, rank):
    return jnp.concatenate([x[i : i + rank] for i in range(0, x.shape[0], rank)], 1)


def in_hbm(x):
    return pltpu.with_memory_space_constraint(x, pltpu.HBM)


def grad_kernel(go_hbm, tok_hbm, fb_hbm, q_hbm, own_ref, other_ref, p_ref, go_v, tok_v, fb_v, q_v, qt_v, sems, *, blocks):
    rank, rows = p_ref.shape
    d = tok_hbm.shape[1]
    width = d // blocks
    core = lax.axis_index("tensor") & 1
    copy_go = pltpu.make_async_copy(go_hbm, go_v, sems.at[0])
    copy_go.start()
    copies_q = []
    for k in range(2):
        there = pl.ds(pl.multiple_of((core ^ k) * (d // 2), d // 2), d // 2)
        copies_q.append(pltpu.make_async_copy(q_hbm.at[:, there], q_v.at[:, pl.ds(k * (d // 2), d // 2)], sems.at[1 + k]))
        copies_q[k].start()
    copies = []
    for k in range(blocks):
        start = (core ^ (2 * k // blocks)) * (d // 2) + k % (blocks // 2) * width
        there = pl.ds(pl.multiple_of(start, width), width)
        block = [
            pltpu.make_async_copy(whole.at[:, there], local.at[:, pl.ds(k * width, width)], sems.at[3 + 2 * k + i])
            for i, (whole, local) in enumerate([(fb_hbm, fb_v), (tok_hbm, tok_v)])
        ]
        for copy in block:
            copy.start()
        copies.append(block)
    copy_go.wait()
    go = go_v[...]
    for copy in copies_q:
        copy.wait()
    for k in range(blocks):
        q2 = jnp.concatenate(split2(q_v[:, k * width : (k + 1) * width]), 0)
        qt_v[k * width : (k + 1) * width, :] = q2.T
    total = None
    for k in range(blocks):
        for copy in copies[k]:
            copy.wait()
        part = pl.ds(k * width, width)
        merged = dot(go, tok_v[:, part], NN) + fb_v[:, part].astype(jnp.float32)
        half_ref = own_ref if 2 * k < blocks else other_ref
        half_ref[:, pl.ds(k % (blocks // 2) * width, width)] = merged
        term = dot(jnp.concatenate(split2(merged), 0), qt_v[part, :], NN)
        total = term if total is None else total + term
    total = total[:, :rank] + total[:, rank:]
    p_ref[...] = (total[:rows] + total[rows:]).T


def place_of(chunk, h, side):
    dp, tensor = lax.axis_index("dp"), lax.axis_index("tensor")
    x, y, z = dp & 1, (dp // side) & 1, (tensor >> 1) & 1
    return (y ^ (chunk >> 1)) * 4 + (x ^ (chunk & 1)) * 2 + (z ^ h)


def z_kernel(p_ref, merged_ref, *refs, chunks, piece, side):
    z_ref = refs[-1]
    rank, rows = p_ref.shape
    p = p_ref[...]
    hi, lo = split2(p)
    p2 = jnp.concatenate([jnp.concatenate([hi, hi], 1), jnp.concatenate([lo, lo], 1)], 0)

    def put(start, width, value):
        z_ref[:, start : start + width] = value + refs[0][:, start : start + width] if len(refs) > 1 else value

    for k in range(2 * len(chunks)):
        start = pl.multiple_of(place_of(chunks[k // 2], k % 2, side) * piece, piece)
        m2 = merged_ref[:, pl.ds(start, piece)]
        if m2.dtype == jnp.float32:
            m2 = jnp.concatenate(split2(m2), 0)
        part = dot(p2, m2, NN)
        put(k * piece, piece, part[:rank] + part[rank:])


def gram_kernel(p_ref, sibling_ref, gram_ref):
    gram_ref[...] = pack(
        sum(
            lax.dot_general(x[...], x[...], NT, precision=HIGHEST, preferred_element_type=jnp.float32)
            for x in (p_ref, sibling_ref)
        )
    )


def split_kernel(merged_ref, parts_ref):
    rows = merged_ref.shape[0]
    hi, lo = split2(merged_ref[...])
    parts_ref[:rows, :] = hi
    parts_ref[rows:, :] = lo


def factor_kernel(gram_ref, p_ref, a_ref, *, replicas):
    rank = p_ref.shape[0]
    gram = unpack(gram_ref[...], rank)
    gram = jnp.concatenate([gram, jnp.zeros((rank, 128 - rank), jnp.float32)], 1)
    lane = lax.broadcasted_iota(jnp.int32, (rank, 128), 1)
    sub = lax.broadcasted_iota(jnp.int32, (rank, 128), 0)
    diagonal = jnp.where(lane == sub, gram, 0.0)
    by_row = 1.0 / jnp.sqrt(jnp.sum(diagonal, 1, keepdims=True))
    by_lane = jnp.where(lane[:1] < rank, 1.0 / jnp.sqrt(jnp.sum(diagonal, 0, keepdims=True)), 0.0)
    work = jnp.where(lane < rank, gram * by_row * by_lane, jnp.where(lane == sub + rank, by_row, 0.0))
    for j in range(0, rank - 2, 2):
        col0 = jnp.broadcast_to(work[:, j : j + 1], (rank, 128))
        col1 = jnp.broadcast_to(work[:, j + 1 : j + 2], (rank, 128))
        row0, row1 = work[j : j + 1, :], work[j + 1 : j + 2, :]
        a, b, c = col0[j : j + 1, :], col1[j : j + 1, :], col1[j + 1 : j + 2, :]
        scale = 1.0 / (a * c - b * b)
        step0, step1 = (c * row0 - b * row1) * scale, (a * row1 - b * row0) * scale
        below = sub > j + 1
        work = work - (jnp.where(below, col0, 0.0) * step0 + jnp.where(below, col1, 0.0) * step1)
    previous = jnp.concatenate([work[:1], work[:-1]], 0)
    low = jnp.sum(jnp.where(lane == sub - 1, work, 0.0), 1, keepdims=True)
    above = jnp.sum(jnp.where(lane == sub - 1, previous, 0.0), 1, keepdims=True)
    work = jnp.where(sub % 2 == 1, work - low / above * previous, work)
    pivots = jnp.sum(jnp.where(lane == sub, work, 0.0), 1, keepdims=True)
    inverse = (work / jnp.sqrt(pivots))[:, rank : 2 * rank]
    p_hat = lax.dot_general(inverse, p_ref[...], NN, precision=HIGHEST, preferred_element_type=jnp.float32)
    approx = lax.dot_general(p_hat, inverse, TN, precision=HIGHEST, preferred_element_type=jnp.float32) / replicas
    hi, lo = split2(jnp.concatenate([inverse, approx], 0))
    a_ref[...] = jnp.concatenate([hi, hi, lo], 1)


def finish_kernel(*refs, parts, earlier, piece, side):
    a_ref, own_ref, other_ref = refs[:3]
    z_refs = refs[3 : 3 + len(parts)]
    q_hbm, update_hbm, feedback_hbm, q_v, update_v, feedback_v, sems = refs[3 + len(parts) + earlier :]
    half = q_hbm.shape[1] // 2
    rank = q_v.shape[0]
    a = a_ref[...]
    copies = []
    k = 0
    for z_ref, (chunks, sibling) in zip(z_refs, parts):
        for h in range(2 * len(chunks)):
            hi, lo = split2(z_ref[:, h * piece : (h + 1) * piece])
            out = dot(a, jnp.concatenate([hi, lo, hi], 0), NN)
            here = pl.ds(k * piece, piece)
            place = place_of(chunks[h // 2], h % 2, side) * piece
            there = pl.ds(pl.multiple_of(((lax.axis_index("tensor") & 1) ^ sibling) * half + place, piece), piece)
            merged_ref = other_ref if sibling else own_ref
            approx = out[rank:]
            q_v[:, here] = out[:rank]
            update_v[:, here] = approx.astype(jnp.bfloat16)
            feedback_v[:, here] = (merged_ref[:, pl.ds(pl.multiple_of(place, piece), piece)] - approx).astype(jnp.bfloat16)
            for i, (local, whole) in enumerate([(q_v, q_hbm), (update_v, update_hbm), (feedback_v, feedback_hbm)]):
                copy = pltpu.make_async_copy(local.at[:, here], whole.at[:, there], sems.at[3 * k + i])
                copy.start()
                copies.append(copy)
            k += 1
    for copy in copies:
        copy.wait()


def grad_call(go, tokens, feedback, q, blocks=4):
    rows, toks = go.shape
    d = tokens.shape[1]
    rank = q.shape[0]
    return pl.pallas_call(
        functools.partial(grad_kernel, blocks=blocks),
        in_specs=[pl.BlockSpec(memory_space=pl.ANY)] * 4,
        out_specs=[pl.BlockSpec(memory_space=pltpu.VMEM)] * 3,
        out_shape=[
            jax.ShapeDtypeStruct((rows, d // 2), jnp.float32),
            jax.ShapeDtypeStruct((rows, d // 2), jnp.float32),
            jax.ShapeDtypeStruct((rank, rows), jnp.float32),
        ],
        scratch_shapes=[
            pltpu.VMEM((rows, toks), go.dtype),
            pltpu.VMEM((toks, d), tokens.dtype),
            pltpu.VMEM((rows, d), feedback.dtype),
            pltpu.VMEM((rank, d), q.dtype),
            pltpu.VMEM((d, 2 * rank), jnp.bfloat16),
            pltpu.SemaphoreType.DMA((3 + 2 * blocks,)),
        ],
        compiler_params=pltpu.CompilerParams(vmem_limit_bytes=24 * MIB),
        name="grad_and_p",
    )(*[in_hbm(x) for x in (go, tokens, feedback, q)])


def z_call(p, merged, chunks, piece, earlier, side, name):
    rank, rows = p.shape
    width = 2 * len(chunks) * piece
    return pl.pallas_call(
        functools.partial(z_kernel, chunks=chunks, piece=piece, side=side),
        in_specs=[pl.BlockSpec(memory_space=pltpu.VMEM)] * (2 + len(earlier)),
        out_specs=pl.BlockSpec(memory_space=pltpu.VMEM),
        out_shape=jax.ShapeDtypeStruct((rank, width), jnp.float32),
        compiler_params=pltpu.CompilerParams(vmem_limit_bytes=16 * MIB),
        cost_estimate=pl.CostEstimate(flops=8 * rank * rows * width, bytes_accessed=2 * MIB, transcendentals=0),
        name=name,
    )(p, merged, *earlier)


def gram_call(p, p_sibling):
    rank = p.shape[0]
    return pl.pallas_call(
        gram_kernel,
        in_specs=[pl.BlockSpec(memory_space=pltpu.VMEM)] * 2,
        out_specs=pl.BlockSpec(memory_space=pltpu.VMEM),
        out_shape=jax.ShapeDtypeStruct((rank * rank // 128, 128), jnp.float32),
        compiler_params=pltpu.CompilerParams(vmem_limit_bytes=8 * MIB),
        cost_estimate=pl.CostEstimate(flops=10**8, bytes_accessed=MIB, transcendentals=0),
        name="gram",
    )(p, p_sibling)


def split_call(merged):
    rows, width = merged.shape
    return pl.pallas_call(
        split_kernel,
        in_specs=[pl.BlockSpec(memory_space=pltpu.VMEM)],
        out_specs=pl.BlockSpec(memory_space=pltpu.VMEM),
        out_shape=jax.ShapeDtypeStruct((2 * rows, width), jnp.bfloat16),
        compiler_params=pltpu.CompilerParams(vmem_limit_bytes=16 * MIB),
        cost_estimate=pl.CostEstimate(flops=10**6, bytes_accessed=3 * MIB, transcendentals=0),
        name="split_sibling_rows",
    )(merged)


def factor_call(gram, p, replicas):
    rank, rows = p.shape
    return pl.pallas_call(
        functools.partial(factor_kernel, replicas=replicas),
        in_specs=[pl.BlockSpec(memory_space=pltpu.VMEM)] * 2,
        out_specs=pl.BlockSpec(memory_space=pltpu.VMEM),
        out_shape=jax.ShapeDtypeStruct((rank + rows, 3 * rank), jnp.bfloat16),
        compiler_params=pltpu.CompilerParams(vmem_limit_bytes=8 * MIB),
        cost_estimate=pl.CostEstimate(flops=10**9, bytes_accessed=8 * MIB, transcendentals=0),
        name="factor",
    )(gram, p)


def finish_call(a, own, other, parts, d, piece, earlier, side, name):
    zs = [z for z, _, _ in parts]
    rank = zs[0].shape[0]
    rows = own.shape[0]
    width = sum(z.shape[1] for z in zs)
    vmem, anywhere = pl.BlockSpec(memory_space=pltpu.VMEM), pl.BlockSpec(memory_space=pl.ANY)
    return pl.pallas_call(
        functools.partial(
            finish_kernel,
            parts=[(chunks, sibling) for _, chunks, sibling in parts],
            earlier=len(earlier),
            piece=piece,
            side=side,
        ),
        in_specs=[vmem] * (3 + len(zs)) + [anywhere] * len(earlier),
        out_specs=[pl.BlockSpec(memory_space=pltpu.HBM)] * 3,
        out_shape=[
            jax.ShapeDtypeStruct((rank, d), jnp.float32),
            jax.ShapeDtypeStruct((rows, d), jnp.bfloat16),
            jax.ShapeDtypeStruct((rows, d), jnp.bfloat16),
        ],
        scratch_shapes=[
            pltpu.VMEM((rank, width), jnp.float32),
            pltpu.VMEM((rows, width), jnp.bfloat16),
            pltpu.VMEM((rows, width), jnp.bfloat16),
            pltpu.SemaphoreType.DMA((3 * width // piece,)),
        ],
        input_output_aliases={3 + len(zs) + i: i for i in range(len(earlier))},
        compiler_params=pltpu.CompilerParams(vmem_limit_bytes=16 * MIB),
        cost_estimate=pl.CostEstimate(flops=10**8, bytes_accessed=4 * MIB, transcendentals=0),
        name=name,
    )(a, own, other, *zs, *earlier)


def solution(mesh):
    replicas, shards = mesh.shape["dp"], mesh.shape["tensor"]
    devices = replicas * shards
    side = 1 << ((replicas.bit_length() - 1) // 2)
    core, near_x, near_y, near_z = 1, shards, side * shards, 2
    plane = [0, near_x, near_y, near_x | near_y]
    far_dp = [f * shards for f in (1 << b for b in range(replicas.bit_length() - 1)) if f not in (1, side)]
    far_tensor = [1 << b for b in range(2, shards.bit_length() - 1)]

    def flip(x, mask):
        return lax.ppermute(x, ("dp", "tensor"), [(i, i ^ mask) for i in range(devices)])

    def sum_dp(p):
        if replicas == 4:
            return (p + flip(p, near_x)) + (flip(p, near_y) + flip(p, near_x | near_y))
        for b in range(replicas.bit_length() - 1):
            p = p + flip(p, shards << b)
        return p

    def on_device(tokens, grad_out, feedback, q_prev):
        d = tokens.shape[1]
        chunk, piece = d // 8, d // 16
        own, other, p = grad_call(grad_out.T, tokens, feedback[0], q_prev.T)
        siblings = split_call(flip(other, core))
        p = sum_dp(p)
        p_sibling = flip(p, core)
        z = z_call(p, own, (3,), piece, (), side, "z_own_far")
        rest = z_call(p, own, (0, 2, 1), piece, (), side, "z_own_near")
        z, p_late = lax.optimization_barrier((z_call(p_sibling, siblings, (3,), piece, (z,), side, "z_sibling_far"), p_sibling))
        rest = z_call(p_late, siblings, (0, 2, 1), piece, (rest,), side, "z_sibling_near")
        part = {3: z, **{c: rest[:, k * chunk : (k + 1) * chunk] for k, c in enumerate((0, 2, 1))}}
        rank = z.shape[0]
        gram = gram_call(p, p_sibling)
        near = flip(part[1], plane[1])
        total = (part[0] + near) + (flip(part[2], plane[2]) + flip(part[3], plane[3]))
        size = rank * piece // 128
        given = jnp.concatenate([stack(total[:, piece:]), gram], 0)
        both = jnp.concatenate([stack(total[:, :piece]), gram], 0) + flip(given, near_z)
        total, gram = both[:size], both[size:]
        for mask in far_dp:
            total = total + flip(total, mask)
        both = jnp.concatenate([total, gram], 0)
        for mask in far_tensor:
            both = both + flip(both, mask)
        total, gram = both[:size], both[size:]
        a = factor_call(gram, p, replicas)
        whole = jnp.concatenate([unstack(total, rank), unstack(flip(total, near_z), rank)], 1)
        whole, a = lax.optimization_barrier((whole, a))
        got = {0: whole}
        for k in (3, 2, 1):
            got[k] = flip(whole, plane[k])
        outs = finish_call(a, own, other, [(got[0], (0,), 0), (got[3], (3,), 0)], d, piece, (), side, "finish_first")
        first = flip(jnp.concatenate([got[0], got[3]], 1), core)
        second, outs = lax.optimization_barrier((jnp.concatenate([got[2], got[1]], 1), outs))
        second = flip(second, core)
        outs = finish_call(a, own, other, [(got[2], (2,), 0), (got[1], (1,), 0)], d, piece, outs, side, "finish_second")
        q, update, new_feedback = finish_call(a, own, other, [(first, (0, 3), 1), (second, (2, 1), 1)], d, piece, outs, side, "finish_third")
        return q.T, update, new_feedback[None]

    return jax.shard_map(
        on_device,
        mesh=mesh,
        in_specs=(P("dp", None), P("dp", "tensor"), P("dp", "tensor", None), P()),
        out_specs=(P(), P("tensor", None), P("dp", "tensor", None)),
        check_vma=False,
    )
```
